128 devices in a mesh: seq: 64 (over z, y_hi, x, core), utt: 2 (over y_lo).
Axes of the slice: x: 4, y: 4 (y_hi: 2, y_lo: 2; y = y_hi * 2 + y_lo), z: 4, core: 2. Of those that a mesh axis runs over, the one named last changes fastest.
Arguments:
- inputs: bfloat16 [2, 8192, 1536], P('utt', 'seq'), may hold values from -6 to 6
- attention_norm_gain: float32 [1536], replicated, may hold values from 1.5 to 5.5
- w_query: bfloat16 [1536, 768], replicated, may hold values from -0.15625 to 0.15625
- w_key: bfloat16 [1536, 768], replicated, may hold values from -0.15625 to 0.15625
- w_value: bfloat16 [1536, 768], replicated, may hold values from -0.15625 to 0.15625
- w_out: bfloat16 [768, 1536], replicated, may hold values from -0.21875 to 0.21875
- gain_conv: float32 [1536], replicated, may hold values from 0.25 to 1.75
- kernel: float32 [32, 1536], replicated, may hold values from -1 to 1
- w_point: bfloat16 [1536, 1536], replicated, may hold values from -0.15625 to 0.15625
- cotangent: bfloat16 [2, 8192, 1536], P('utt', 'seq'), may hold values from -6 to 6
Outputs:
- layer_out: bfloat16 [2, 8192, 1536], P('utt', 'seq')
- grad_hidden: bfloat16 [2, 8192, 1536], P('utt', 'seq')
- grad_point: float32 [1536, 1536], P('seq')
- grad_kernel: float32 [32, 1536], replicated
- grad_gain: float32 [1536], replicated
The draws below stay inside these ranges and needn't reach their ends.
All inputs are finite; a program needn't handle non-finite values.
Results may differ from the reference program's by a relative error of at most 0.02.
The reference program's roundings to bfloat16 on the way count: a program that leaves them out, or rounds other values in their place, can miss the bound.
Values may be sent and summed in bfloat16 or wider, within the bound.
A program may use at most 192 MiB of HBM per device.

```python
import math
import jax
import jax.numpy as jnp
from jax import lax

D = 1536
HEADS = 8
HEAD_DIM = 96
KER = 32
FRAMES = 8192
RECS = 2


def draw_attention_norm_gain(key, part):
    key = jax.random.fold_in(key, 11)
    return jnp.exp(jax.random.uniform(key, (D,), jnp.float32, math.log(1.5), math.log(3.0)))


def levels(rng, dims, split, smallest, top_value):
    def one(position, shards_of):
        steps = jax.random.uniform(jax.random.fold_in(jax.random.fold_in(rng, 6), position), (shards_of,), jnp.float32, smallest / len(split), top_value / len(split))
        return jnp.repeat(jnp.exp(steps), dims[position] // shards_of).reshape((-1,) + (1,) * (len(dims) - position - 1))

    loudness = one(*split[0])
    for cut in split[1:]:
        loudness = loudness * one(*cut)
    return loudness


def centred(rng, extent, width, reach, cuts=(), kind=jnp.bfloat16):
    array = width * jax.random.normal(rng, extent, jnp.float32)
    if cuts:
        array = array * levels(rng, extent, cuts, -0.22, 0.18)
    return jnp.clip(array, -reach, reach).astype(kind)


def setup_inputs(seed: int = 0) -> dict:
    key_of = jax.random.split(jax.random.key(seed), 11)
    inputs = centred(key_of[0], (RECS, FRAMES, D), 1.0, 6.0, ((0, 2), (1, 64)))
    attention_norm_gain = draw_attention_norm_gain(jax.random.fold_in(key_of[10], 71), 0)
    w_query = centred(key_of[2], (D, HEADS * HEAD_DIM), D ** -0.5, 0.15625)
    w_key = centred(key_of[3], (D, HEADS * HEAD_DIM), D ** -0.5, 0.15625)
    w_value = centred(key_of[4], (D, HEADS * HEAD_DIM), D ** -0.5, 0.15625)
    w_out = centred(key_of[5], (HEADS * HEAD_DIM, D), (HEADS * HEAD_DIM) ** -0.5, 0.21875)
    gain_conv = jnp.clip(1.0 + 0.15 * jax.random.normal(key_of[6], (D,), jnp.float32), 0.25, 1.75)
    kernel = centred(key_of[7], (KER, D), KER ** -0.5, 1.0, (), jnp.float32)
    w_point = centred(key_of[8], (D, D), D ** -0.5, 0.15625)
    cotangent = centred(key_of[9], (RECS, FRAMES, D), 1.0, 6.0, ((0, 2), (1, 64)))
    return {"inputs": inputs, "attention_norm_gain": attention_norm_gain, "w_query": w_query, "w_key": w_key, "w_value": w_value, "w_out": w_out, "gain_conv": gain_conv, "kernel": kernel, "w_point": w_point, "cotangent": cotangent}


def standardize_rows(values):
    mean = lax.optimization_barrier(jnp.mean(values, axis=-1, keepdims=True))
    centered = values - mean
    rstd = lax.rsqrt(lax.optimization_barrier(jnp.mean(centered * centered, axis=-1, keepdims=True)) + 1e-05)
    return (centered * rstd, rstd)

def attend(queries, keys, values):
    frames = queries.shape[0]
    block = math.gcd(frames, 256)
    key_heads = keys.reshape(frames, HEADS, HEAD_DIM).astype(jnp.float32)
    value_heads = values.reshape(frames, HEADS, HEAD_DIM).astype(jnp.float32)
    query_blocks = queries.reshape(frames // block, block, HEADS, HEAD_DIM)
    scale = 1.0 / math.sqrt(HEAD_DIM)

    def one_block(query_block):
        scores = jnp.einsum('bhd,fhd->hbf', query_block.astype(jnp.float32), key_heads) * scale
        top = lax.optimization_barrier(jnp.max(scores, axis=-1, keepdims=True))
        expo = jnp.exp(scores - top)
        total = lax.optimization_barrier(jnp.sum(expo, axis=-1))
        weights = lax.optimization_barrier(expo.astype(jnp.bfloat16))
        summed = jnp.einsum('hbf,fhd->bhd', weights.astype(jnp.float32), value_heads)
        return (summed / total.T[:, :, None]).reshape(block, HEADS * HEAD_DIM).astype(jnp.bfloat16)
    return lax.map(one_block, query_blocks).reshape(frames, HEADS * HEAD_DIM)

def reference(inputs, attention_norm_gain, w_query, w_key, w_value, w_out, gain_conv, kernel, w_point, cotangent):
    half = KER // 2
    frames = inputs.shape[1]
    scale = 1.0 / math.sqrt(RECS * FRAMES)
    outs, grads_in = ([], [])
    grad_point = jnp.zeros((D, D), jnp.float32)
    grad_kernel = jnp.zeros((KER, D), jnp.float32)
    grad_gain = jnp.zeros((D,), jnp.float32)
    for record in range(RECS):
        input_frames = inputs[record].astype(jnp.float32)
        standardized_input, unused_item = standardize_rows(input_frames)
        normed_rows = (standardized_input * attention_norm_gain).astype(jnp.bfloat16)
        queries = jnp.dot(normed_rows, w_query, preferred_element_type=jnp.float32).astype(jnp.bfloat16)
        keys = jnp.dot(normed_rows, w_key, preferred_element_type=jnp.float32).astype(jnp.bfloat16)
        values = jnp.dot(normed_rows, w_value, preferred_element_type=jnp.float32).astype(jnp.bfloat16)
        mixed = attend(queries, keys, values)
        hidden = (input_frames + jnp.dot(mixed, w_out, preferred_element_type=jnp.float32)).astype(jnp.bfloat16)
        hidden_f = hidden.astype(jnp.float32)
        hhat, rstd = standardize_rows(hidden_f)
        conv_in = (hhat * gain_conv).astype(jnp.bfloat16)
        padded = jnp.pad(conv_in.astype(jnp.float32), ((half, KER - 1 - half), (0, 0)))
        conv = jnp.zeros((frames, D), jnp.float32)
        for tap in range(KER):
            conv = conv + kernel[tap] * padded[tap:tap + frames]
        act = (conv * jax.nn.sigmoid(conv)).astype(jnp.bfloat16)
        outs.append((hidden_f + jnp.dot(act, w_point, preferred_element_type=jnp.float32)).astype(jnp.bfloat16))
        grad_now = cotangent[record]
        grad_point = grad_point + lax.dot_general(act, grad_now, (((0,), (0,)), ((), ())), preferred_element_type=jnp.float32)
        back = lax.dot_general(grad_now, w_point, (((1,), (1,)), ((), ())), preferred_element_type=jnp.float32)
        sig = jax.nn.sigmoid(conv)
        dz = back * sig * (1.0 + conv * (1.0 - sig))
        grad_kernel = grad_kernel + jnp.stack([lax.optimization_barrier(jnp.sum(dz * padded[tap:tap + frames], axis=0)) for tap in range(KER)])
        dz_pad = jnp.pad(dz, ((KER - 1 - half, half), (0, 0)))
        dconv_in = jnp.zeros((frames, D), jnp.float32)
        for tap in range(KER):
            dconv_in = dconv_in + kernel[tap] * dz_pad[KER - 1 - tap:KER - 1 - tap + frames]
        grad_gain = grad_gain + lax.optimization_barrier(jnp.sum(dconv_in * hhat, axis=0))
        scaled = dconv_in * gain_conv
        inner = scaled - lax.optimization_barrier(jnp.mean(scaled, axis=-1, keepdims=True)) - hhat * lax.optimization_barrier(jnp.mean(scaled * hhat, axis=-1, keepdims=True))
        grads_in.append((grad_now.astype(jnp.float32) + rstd * inner).astype(jnp.bfloat16))
    return (jnp.stack(outs), jnp.stack(grads_in), grad_point * scale, grad_kernel * scale, grad_gain * scale)
```

```python
import math

import jax
import jax.numpy as jnp
from jax import lax
from jax.experimental import pallas as pl
from jax.experimental.pallas import tpu as pltpu
from jax.sharding import PartitionSpec as P

D = 1536
HEADS = 8
HEAD_DIM = 96
WIDE = HEADS * HEAD_DIM
KER = 32
BLOCK = 128
HALF = 512
LOG2E = 1.4426950408889634

OWN, SIB, ZM, ZP, Z2, SIB_ZM, SIB_ZP, SIB_Z2 = range(8)


def rows_norm(values):
    mean = jnp.mean(values, axis=-1, keepdims=True)
    centered = values - mean
    rstd = lax.rsqrt(jnp.mean(centered * centered, axis=-1, keepdims=True) + 1e-05)
    return centered * rstd, rstd


def matmul(a, b, da=1, db=0):
    return lax.dot_general(a, b, (((da,), (db,)), ((), ())), preferred_element_type=jnp.float32)


def attention_kernel(
    x_ref, gain_ref, wk_hbm, wv_hbm, wq_hbm, wo_hbm,
    hidden_ref,
    wk, wv, wq, wo, normed, kv_out, q_out, kv, qt, acc, top, mix_out, mixt,
    wsem, kv_send, kv_recv, q_send, q_recv, m_send, m_recv, r_send, r_recv, lsem,
):
    s = lax.axis_index("seq")
    z = s // 16
    h = (s % 16) // 2
    c = s % 2

    def dev(zz, hh, cc):
        return {"seq": zz * 16 + hh * 2 + cc}

    peers = [dev(z, (h + k) % 8, c) for k in range(1, 8)]
    up, down = dev((z + 1) % 4, h, c), dev((z + 3) % 4, h, c)
    sibling = dev(z, h, 1 - c)

    def remote(src, dst, send, recv, to):
        copy = pltpu.make_async_remote_copy(
            src_ref=src, dst_ref=dst, send_sem=send, recv_sem=recv,
            device_id=to, device_id_type=pl.DeviceIdType.MESH,
        )
        copy.start()
        return copy

    loads = [
        pltpu.make_async_copy(src, dst, wsem.at[i])
        for i, (src, dst) in enumerate(((wk_hbm, wk), (wv_hbm, wv), (wq_hbm, wq), (wo_hbm, wo)))
    ]
    for load in loads:
        load.start()
    for slot in range(16):
        kv[slot, 192:208, :] = jnp.ones((16, HALF), jnp.bfloat16)

    barrier = pltpu.get_barrier_semaphore()
    for to in peers + [up, down, sibling]:
        pl.semaphore_signal(barrier, inc=1, device_id=to, device_id_type=pl.DeviceIdType.MESH)

    xhat, unused_item = rows_norm(x_ref[...].astype(jnp.float32))
    normed[...] = (xhat * gain_ref[...]).astype(jnp.bfloat16)
    loads[0].wait()
    k_rows = matmul(normed[...], wk[...]).T.astype(jnp.bfloat16)
    for i in range(HEADS):
        kv_out[i, 0:96, :] = k_rows[i * 96 : i * 96 + 96, :]
    loads[1].wait()
    v_rows = matmul(normed[...], wv[...]).T.astype(jnp.bfloat16)
    for i in range(HEADS):
        kv_out[i, 96:192, :] = v_rows[i * 96 : i * 96 + 96, :]

    pl.semaphore_wait(barrier, 10)
    mine = pl.ds(pl.multiple_of((h % 4) * 128, 128), 128)
    kv_copies = [
        remote(kv_out.at[(h + k) % 8], kv.at[h // 4, 0:192, mine],
               kv_send.at[k - 1], kv_recv.at[k - 1], peers[k - 1])
        for k in range(1, 8)
    ]
    kv_self = pltpu.make_async_copy(kv_out.at[h], kv.at[h // 4, 0:192, mine], lsem.at[0])
    kv_self.start()

    loads[2].wait()
    scale = LOG2E / math.sqrt(HEAD_DIM)
    q_rows = (matmul(normed[...], wq[...]) * scale).T.astype(jnp.bfloat16)
    for i in range(HEADS):
        q_out[i] = q_rows[i * 96 : i * 96 + 96, :]
    lanes = pl.ds(pl.multiple_of(h * 128, 128), 128)
    q_copies = [
        remote(q_out.at[(h + k) % 8], qt.at[:, lanes],
               q_send.at[k - 1], q_recv.at[k - 1], peers[k - 1])
        for k in range(1, 8)
    ]
    q_self = pltpu.make_async_copy(q_out.at[h], qt.at[:, lanes], lsem.at[1])
    q_self.start()

    sent = []

    def forward(slot, half, to, to_slot):
        sem = len(sent)
        copy = remote(kv.at[2 * slot + half, 0:192], kv.at[2 * to_slot + half, 0:192],
                      r_send.at[sem], r_recv.at[sem], to)
        sent.append(copy)
        return copy

    acc[...] = jnp.zeros_like(acc)
    top[...] = jnp.full_like(top, -1e30)

    def attend(*halves):
        halves = [2 * slot + half for slot, half in halves]
        scores = [matmul(kv[i, 0:96, :], qt[...], 0, 0) for i in halves]
        before = top[0:1, :]
        newest = before
        for part in scores:
            newest = jnp.maximum(newest, jnp.max(part, axis=0, keepdims=True))
        total = acc[...] * jnp.exp2(before - newest)
        for i, part in zip(halves, scores):
            total += matmul(kv[i, 96:208, :], jnp.exp2(part - newest).astype(jnp.bfloat16))
        acc[...] = total
        top[0:1, :] = newest

    for copy in kv_copies:
        copy.wait_recv()
    kv_self.wait()
    zm0 = forward(OWN, 0, up, ZM)
    zp1 = forward(OWN, 1, down, ZP)
    sib0 = forward(OWN, 0, sibling, SIB)
    sib1 = forward(OWN, 1, sibling, SIB)
    zm1 = forward(OWN, 1, up, ZM)
    zp0 = forward(OWN, 0, down, ZP)
    for copy in q_copies:
        copy.wait_recv()
    q_self.wait()
    attend((OWN, 0), (OWN, 1))
    zm0.wait_recv()
    z20 = forward(ZM, 0, up, Z2)
    szm0 = forward(ZM, 0, sibling, SIB_ZM)
    zp1.wait_recv()
    z21 = forward(ZP, 1, down, Z2)
    szp1 = forward(ZP, 1, sibling, SIB_ZP)
    sib0.wait_recv()
    sib1.wait_recv()
    attend((SIB, 0), (SIB, 1), (ZM, 0), (ZP, 1))
    zm1.wait_recv()
    szm1 = forward(ZM, 1, sibling, SIB_ZM)
    zp0.wait_recv()
    szp0 = forward(ZP, 0, sibling, SIB_ZP)
    szm0.wait_recv()
    szp1.wait_recv()
    attend((SIB_ZM, 0), (SIB_ZP, 1), (ZM, 1), (ZP, 0))
    z20.wait_recv()
    sz20 = forward(Z2, 0, sibling, SIB_Z2)
    z21.wait_recv()
    sz21 = forward(Z2, 1, sibling, SIB_Z2)
    szm1.wait_recv()
    szp0.wait_recv()
    attend((SIB_ZM, 1), (SIB_ZP, 0), (Z2, 0), (Z2, 1))
    sz20.wait_recv()
    sz21.wait_recv()
    attend((SIB_Z2, 0), (SIB_Z2, 1))

    mix_out[...] = (acc[0:96, :] / acc[96:97, :]).astype(jnp.bfloat16)
    band = pl.ds(pl.multiple_of(h * 96, 96), 96)
    m_copies = []
    for k in range(1, 8):
        to_lanes = pl.ds(pl.multiple_of(((h + k) % 8) * 128, 128), 128)
        m_copies.append(
            remote(mix_out.at[:, to_lanes], mixt.at[band, :],
                   m_send.at[k - 1], m_recv.at[k - 1], peers[k - 1])
        )
    m_self = pltpu.make_async_copy(mix_out.at[:, lanes], mixt.at[band, :], lsem.at[2])
    m_self.start()
    loads[3].wait()
    for copy in m_copies:
        copy.wait_recv()
    m_self.wait()
    hidden_ref[...] = (x_ref[...].astype(jnp.float32) + matmul(mixt[...], wo[...], 0, 0)).astype(
        jnp.bfloat16
    )
    for copy in kv_copies + q_copies + sent + m_copies:
        copy.wait_send()


def attention(x, gain, w_key, w_value, w_query, w_out):
    bf = jnp.bfloat16
    vmem = pl.BlockSpec(memory_space=pltpu.VMEM)
    hbm = pl.BlockSpec(memory_space=pl.ANY)
    dma = pltpu.SemaphoreType.DMA
    return pl.pallas_call(
        attention_kernel,
        name="attention",
        out_shape=jax.ShapeDtypeStruct((BLOCK, D), bf),
        in_specs=[vmem, vmem, hbm, hbm, hbm, hbm],
        out_specs=vmem,
        scratch_shapes=[
            pltpu.VMEM((D, WIDE), bf),
            pltpu.VMEM((D, WIDE), bf),
            pltpu.VMEM((D, WIDE), bf),
            pltpu.VMEM((WIDE, D), bf),
            pltpu.VMEM((BLOCK, D), bf),
            pltpu.VMEM((HEADS, 192, 128), bf),
            pltpu.VMEM((HEADS, 96, 128), bf),
            pltpu.VMEM((16, 208, HALF), bf),
            pltpu.VMEM((96, 1024), bf),
            pltpu.VMEM((112, 1024), jnp.float32),
            pltpu.VMEM((8, 1024), jnp.float32),
            pltpu.VMEM((96, 1024), bf),
            pltpu.VMEM((WIDE, 128), bf),
            dma((4,)), dma((7,)), dma((7,)), dma((7,)), dma((7,)), dma((7,)), dma((7,)),
            dma((14,)), dma((14,)), dma((3,)),
        ],
        compiler_params=pltpu.CompilerParams(
            collective_id=0, has_side_effects=True, vmem_limit_bytes=48 << 20
        ),
        cost_estimate=pl.CostEstimate(
            flops=6 * 10**9, bytes_accessed=10 * 2**20, transcendentals=2**23
        ),
    )(x, gain, w_key, w_value, w_query, w_out)


def with_halo(block, sides, width):
    for axis, dim in sides:
        count = lax.axis_size(axis)
        forward = [(i, i + 1) for i in range(count - 1)]
        backward = [(target, source) for source, target in forward]
        low = lax.ppermute(
            lax.slice_in_dim(block, block.shape[dim] - width, None, axis=dim), axis, forward
        )
        high = lax.ppermute(lax.slice_in_dim(block, 0, width, axis=dim), axis, backward)
        block = jnp.concatenate([low, block, high], axis=dim)
    return block


def standardize_rows(values):
    mean = jnp.mean(values, axis=-1, keepdims=True)
    centered = values - mean
    rstd = lax.rsqrt(jnp.mean(centered * centered, axis=-1, keepdims=True) + 1e-05)
    return (centered * rstd, rstd)


def depthwise(source, kernel, count):
    result = jnp.zeros((count, source.shape[1]), jnp.float32)
    for tap in range(kernel.shape[0]):
        result = result + kernel[tap] * source[tap : tap + count].astype(jnp.float32)
    return result


def swish_grad(values):
    sig = jax.nn.sigmoid(values)
    return sig * (1.0 + values * (1.0 - sig))


def on_device(
    inputs,
    attention_norm_gain,
    w_query,
    w_key,
    w_value,
    w_out,
    gain_conv,
    kernel,
    w_point,
    cotangent,
):
    count = inputs.shape[1]
    width = D
    half = KER // 2
    hidden_f = attention(
        inputs[0], attention_norm_gain[None], w_key, w_value, w_query, w_out
    ).astype(jnp.float32)
    hhat, rstd = standardize_rows(hidden_f)
    conv_in = (hhat * gain_conv).astype(jnp.bfloat16)
    grad_now = cotangent[0]
    taps_source = with_halo(conv_in, (("seq", 0),), half)
    conv = depthwise(taps_source, kernel, count)
    back = lax.dot_general(
        grad_now, w_point, (((1,), (1,)), ((), ())), preferred_element_type=jnp.float32
    )
    dz = back * swish_grad(conv)
    dz_pad = with_halo(dz.astype(jnp.bfloat16), (("seq", 0),), half).astype(dz.dtype)
    act = (conv * jax.nn.sigmoid(conv)).astype(jnp.bfloat16)
    layer_out = (hidden_f + jnp.dot(act, w_point, preferred_element_type=jnp.float32)).astype(
        jnp.bfloat16
    )
    taps_f = taps_source.astype(jnp.float32)
    local_kernel = jnp.stack(
        [jnp.sum(dz * taps_f[tap : tap + count], axis=0) for tap in range(KER)]
    )
    dconv_in = jnp.zeros((count, width), jnp.float32)
    for tap in range(KER):
        dconv_in = dconv_in + kernel[tap] * dz_pad[2 * half - tap : 2 * half - tap + count]
    local_gain = jnp.sum(dconv_in * hhat, axis=0)
    scaled = dconv_in * gain_conv
    inner = (
        scaled
        - jnp.mean(scaled, axis=-1, keepdims=True)
        - hhat * jnp.mean(scaled * hhat, axis=-1, keepdims=True)
    )
    grad_hidden = (grad_now.astype(jnp.float32) + rstd * inner).astype(jnp.bfloat16)
    grad_scale = 1.0 / math.sqrt(lax.axis_size("utt") * lax.axis_size("seq") * count)
    summed_kernel, summed_gain = lax.psum((local_kernel, local_gain), ("seq", "utt"))
    shares = lax.psum_scatter(
        lax.dot_general(
            act, grad_now, (((0,), (0,)), ((), ())), preferred_element_type=jnp.float32
        ),
        "seq",
        scatter_dimension=0,
        tiled=True,
    )
    grad_point = lax.psum(shares.astype(jnp.bfloat16), "utt").astype(jnp.float32)
    return (
        layer_out[None],
        grad_hidden[None],
        grad_point * grad_scale,
        summed_kernel * grad_scale,
        summed_gain * grad_scale,
    )


def solution(mesh):
    placed = (P("utt", "seq", None), P(), P(), P(), P(), P(), P(), P(), P(), P("utt", "seq", None))
    return jax.shard_map(
        on_device,
        mesh=mesh,
        in_specs=placed,
        out_specs=(P("utt", "seq", None), P("utt", "seq", None), P("seq", None), P(), P()),
        check_vma=False,
    )
```

```python
import math

import jax
import jax.numpy as jnp
from jax import lax
from jax.experimental import pallas as pl
from jax.experimental.pallas import tpu as pltpu
from jax.sharding import PartitionSpec as P

D = 1536
HEADS = 8
HEAD_DIM = 96
WIDE = HEADS * HEAD_DIM
KER = 32
BLOCK = 128
HALF = 512
LOG2E = 1.4426950408889634

OWN, SIB, ZM, ZP, Z2, SIB_ZM, SIB_ZP, SIB_Z2 = range(8)


def rows_norm(values):
    mean = jnp.mean(values, axis=-1, keepdims=True)
    centered = values - mean
    rstd = lax.rsqrt(jnp.mean(centered * centered, axis=-1, keepdims=True) + 1e-05)
    return centered * rstd, rstd


def matmul(a, b, da=1, db=0):
    return lax.dot_general(a, b, (((da,), (db,)), ((), ())), preferred_element_type=jnp.float32)


def attention_kernel(
    x_ref, gain_ref, wk_hbm, wv_hbm, wq_hbm, wo_hbm, cot_hbm,
    hidden_ref, cots_hbm,
    wk, wv, wq, wo, normed, kv_out, q_out, kv, qt, acc, top, mix_out, mixt,
    wsem, kv_send, kv_recv, q_send, q_recv, m_send, m_recv, r_send, r_recv, c_send, c_recv, lsem,
):
    s = lax.axis_index("seq")
    z = s // 16
    h = (s % 16) // 2
    c = s % 2

    def dev(zz, hh, cc):
        return {"seq": zz * 16 + hh * 2 + cc}

    peers = [dev(z, (h + k) % 8, c) for k in range(1, 8)]
    up, down = dev((z + 1) % 4, h, c), dev((z + 3) % 4, h, c)
    sibling = dev(z, h, 1 - c)

    def remote(src, dst, send, recv, to):
        copy = pltpu.make_async_remote_copy(
            src_ref=src, dst_ref=dst, send_sem=send, recv_sem=recv,
            device_id=to, device_id_type=pl.DeviceIdType.MESH,
        )
        copy.start()
        return copy

    loads = [
        pltpu.make_async_copy(src, dst, wsem.at[i])
        for i, (src, dst) in enumerate(((wk_hbm, wk), (wv_hbm, wv), (wq_hbm, wq), (wo_hbm, wo)))
    ]
    for load in loads:
        load.start()
    for slot in range(16):
        kv[slot, 192:208, :] = jnp.ones((16, HALF), jnp.bfloat16)

    barrier = pltpu.get_barrier_semaphore()
    for to in peers + [up, down, sibling]:
        pl.semaphore_signal(barrier, inc=1, device_id=to, device_id_type=pl.DeviceIdType.MESH)

    xhat, unused_item = rows_norm(x_ref[...].astype(jnp.float32))
    normed[...] = (xhat * gain_ref[...]).astype(jnp.bfloat16)
    loads[0].wait()
    k_rows = matmul(normed[...], wk[...]).T.astype(jnp.bfloat16)
    for i in range(HEADS):
        kv_out[i, 0:96, :] = k_rows[i * 96 : i * 96 + 96, :]
    loads[1].wait()
    v_rows = matmul(normed[...], wv[...]).T.astype(jnp.bfloat16)
    for i in range(HEADS):
        kv_out[i, 96:192, :] = v_rows[i * 96 : i * 96 + 96, :]

    pl.semaphore_wait(barrier, 10)
    mine = pl.ds(pl.multiple_of((h % 4) * 128, 128), 128)
    kv_copies = [
        remote(kv_out.at[(h + k) % 8], kv.at[h // 4, 0:192, mine],
               kv_send.at[k - 1], kv_recv.at[k - 1], peers[k - 1])
        for k in range(1, 8)
    ]
    kv_self = pltpu.make_async_copy(kv_out.at[h], kv.at[h // 4, 0:192, mine], lsem.at[0])
    kv_self.start()

    loads[2].wait()
    scale = LOG2E / math.sqrt(HEAD_DIM)
    q_rows = (matmul(normed[...], wq[...]) * scale).T.astype(jnp.bfloat16)
    for i in range(HEADS):
        q_out[i] = q_rows[i * 96 : i * 96 + 96, :]
    lanes = pl.ds(pl.multiple_of(h * 128, 128), 128)
    q_copies = [
        remote(q_out.at[(h + k) % 8], qt.at[:, lanes],
               q_send.at[k - 1], q_recv.at[k - 1], peers[k - 1])
        for k in range(1, 8)
    ]
    q_self = pltpu.make_async_copy(q_out.at[h], qt.at[:, lanes], lsem.at[1])
    q_self.start()

    sent = []

    def forward(slot, half, to, to_slot):
        sem = len(sent)
        copy = remote(kv.at[2 * slot + half, 0:192], kv.at[2 * to_slot + half, 0:192],
                      r_send.at[sem], r_recv.at[sem], to)
        sent.append(copy)
        return copy

    acc[...] = jnp.zeros_like(acc)
    top[...] = jnp.full_like(top, -1e30)

    def attend(*halves):
        halves = [2 * slot + half for slot, half in halves]
        scores = [matmul(kv[i, 0:96, :], qt[...], 0, 0) for i in halves]
        before = top[0:1, :]
        newest = before
        for part in scores:
            newest = jnp.maximum(newest, jnp.max(part, axis=0, keepdims=True))
        total = acc[...] * jnp.exp2(before - newest)
        for i, part in zip(halves, scores):
            total += matmul(kv[i, 96:208, :], jnp.exp2(part - newest).astype(jnp.bfloat16))
        acc[...] = total
        top[0:1, :] = newest

    for copy in kv_copies:
        copy.wait_recv()
    kv_self.wait()
    zm0 = forward(OWN, 0, up, ZM)
    zp1 = forward(OWN, 1, down, ZP)
    sib0 = forward(OWN, 0, sibling, SIB)
    sib1 = forward(OWN, 1, sibling, SIB)
    zm1 = forward(OWN, 1, up, ZM)
    zp0 = forward(OWN, 0, down, ZP)
    x, side = h % 4, h // 4
    own_rows = pl.ds(pl.multiple_of((x * 2 + c) * BLOCK, BLOCK), BLOCK)
    c_self = pltpu.make_async_copy(cot_hbm, cots_hbm.at[own_rows], lsem.at[3])
    c_self.start()
    c_copies = [
        remote(cot_hbm, cots_hbm.at[own_rows], c_send.at[k - 1], c_recv.at[k - 1],
               dev(z, side * 4 + (x + k) % 4, c))
        for k in range(1, 4)
    ]
    c_copies.append(
        remote(cot_hbm, cots_hbm.at[own_rows], c_send.at[3], c_recv.at[3], sibling)
    )
    for copy in q_copies:
        copy.wait_recv()
    q_self.wait()
    attend((OWN, 0), (OWN, 1))
    zm0.wait_recv()
    z20 = forward(ZM, 0, up, Z2)
    szm0 = forward(ZM, 0, sibling, SIB_ZM)
    zp1.wait_recv()
    z21 = forward(ZP, 1, down, Z2)
    szp1 = forward(ZP, 1, sibling, SIB_ZP)
    sib0.wait_recv()
    sib1.wait_recv()
    attend((SIB, 0), (SIB, 1), (ZM, 0), (ZP, 1))
    zm1.wait_recv()
    szm1 = forward(ZM, 1, sibling, SIB_ZM)
    zp0.wait_recv()
    szp0 = forward(ZP, 0, sibling, SIB_ZP)
    szm0.wait_recv()
    szp1.wait_recv()
    attend((SIB_ZM, 0), (SIB_ZP, 1), (ZM, 1), (ZP, 0))
    z20.wait_recv()
    sz20 = forward(Z2, 0, sibling, SIB_Z2)
    z21.wait_recv()
    sz21 = forward(Z2, 1, sibling, SIB_Z2)
    szm1.wait_recv()
    szp0.wait_recv()
    for k in range(1, 4):
        c_copies[k - 1].wait_recv()
        rows = pl.ds(pl.multiple_of(((x + 4 - k) % 4 * 2 + c) * BLOCK, BLOCK), BLOCK)
        c_copies.append(
            remote(cots_hbm.at[rows], cots_hbm.at[rows], c_send.at[3 + k], c_recv.at[3 + k], sibling)
        )
    attend((SIB_ZM, 1), (SIB_ZP, 0), (Z2, 0), (Z2, 1))
    sz20.wait_recv()
    sz21.wait_recv()
    attend((SIB_Z2, 0), (SIB_Z2, 1))

    mix_out[...] = (acc[0:96, :] / acc[96:97, :]).astype(jnp.bfloat16)
    band = pl.ds(pl.multiple_of(h * 96, 96), 96)
    m_copies = []
    for k in range(1, 8):
        to_lanes = pl.ds(pl.multiple_of(((h + k) % 8) * 128, 128), 128)
        m_copies.append(
            remote(mix_out.at[:, to_lanes], mixt.at[band, :],
                   m_send.at[k - 1], m_recv.at[k - 1], peers[k - 1])
        )
    m_self = pltpu.make_async_copy(mix_out.at[:, lanes], mixt.at[band, :], lsem.at[2])
    m_self.start()
    loads[3].wait()
    for copy in m_copies:
        copy.wait_recv()
    m_self.wait()
    hidden_ref[...] = (x_ref[...].astype(jnp.float32) + matmul(mixt[...], wo[...], 0, 0)).astype(
        jnp.bfloat16
    )
    for copy in c_copies[3:]:
        copy.wait_recv()
    c_self.wait()
    for copy in kv_copies + q_copies + sent + m_copies + c_copies:
        copy.wait_send()


def attention(x, gain, w_key, w_value, w_query, w_out, cot):
    bf = jnp.bfloat16
    vmem = pl.BlockSpec(memory_space=pltpu.VMEM)
    hbm = pl.BlockSpec(memory_space=pl.ANY)
    dma = pltpu.SemaphoreType.DMA
    return pl.pallas_call(
        attention_kernel,
        name="attention",
        out_shape=(jax.ShapeDtypeStruct((BLOCK, D), bf), jax.ShapeDtypeStruct((8 * BLOCK, D), bf)),
        in_specs=[vmem, vmem, hbm, hbm, hbm, hbm, hbm],
        out_specs=(vmem, hbm),
        scratch_shapes=[
            pltpu.VMEM((D, WIDE), bf),
            pltpu.VMEM((D, WIDE), bf),
            pltpu.VMEM((D, WIDE), bf),
            pltpu.VMEM((WIDE, D), bf),
            pltpu.VMEM((BLOCK, D), bf),
            pltpu.VMEM((HEADS, 192, 128), bf),
            pltpu.VMEM((HEADS, 96, 128), bf),
            pltpu.VMEM((16, 208, HALF), bf),
            pltpu.VMEM((96, 1024), bf),
            pltpu.VMEM((112, 1024), jnp.float32),
            pltpu.VMEM((8, 1024), jnp.float32),
            pltpu.VMEM((96, 1024), bf),
            pltpu.VMEM((WIDE, 128), bf),
            dma((4,)), dma((7,)), dma((7,)), dma((7,)), dma((7,)), dma((7,)), dma((7,)),
            dma((14,)), dma((14,)), dma((7,)), dma((7,)), dma((4,)),
        ],
        compiler_params=pltpu.CompilerParams(
            collective_id=0, has_side_effects=True, vmem_limit_bytes=60 << 20
        ),
        cost_estimate=pl.CostEstimate(
            flops=6 * 10**9, bytes_accessed=10 * 2**20, transcendentals=2**23
        ),
    )(x, gain, w_key, w_value, w_query, w_out, cot)


def conv_kernel(
    hidden_ref, gain_ref, taps_ref, wp_hbm, cot_ref, cots_hbm,
    out_ref, gh_ref, gp_ref, gk_ref, gg_ref,
    wp, cots, hhat, ci, back, dz, act, act_t, act_out, act_in, edge, far, tile_out, tile_in,
    y_out, y_in, part, sums, b_in, c_in, d_in, total,
    lsem, e_send, e_recv, a_send, a_recv, b_send, b_recv, c_send, c_recv, d_send, d_recv,
    g_send, g_recv, t_send, t_recv, y_send, y_recv,
):
    f32, bf = jnp.float32, jnp.bfloat16
    s = lax.axis_index("seq")
    u = lax.axis_index("utt")
    z, y_hi, x, c = s // 16, (s // 8) % 2, (s // 2) % 4, s % 2
    p, y = s % 8, y_hi * 2 + u
    right, left = {"seq": (s + 1) % 64}, {"seq": (s + 63) % 64}
    group = [{"seq": s // 8 * 8 + (p + k) % 8} for k in range(1, 8)]
    z_peers = [{"seq": (z + k) % 4 * 16 + s % 16} for k in range(1, 4)]
    y_peers = [
        {"seq": z * 16 + (y + k) % 4 // 2 * 8 + p, "utt": (y + k) % 4 % 2} for k in range(1, 4)
    ]
    copies = []

    def remote(src, dst, send, recv, to):
        copy = pltpu.make_async_remote_copy(
            src_ref=src, dst_ref=dst, send_sem=send, recv_sem=recv,
            device_id=to, device_id_type=pl.DeviceIdType.MESH,
        )
        copy.start()
        copies.append(copy)
        return copy

    wp_load = pltpu.make_async_copy(wp_hbm, wp, lsem.at[0])
    wp_load.start()
    cots_load = pltpu.make_async_copy(cots_hbm, cots, lsem.at[1])
    cots_load.start()
    barrier = pltpu.get_barrier_semaphore()
    for to in [right, left] + group + z_peers + y_peers:
        pl.semaphore_signal(barrier, inc=1, device_id=to, device_id_type=pl.DeviceIdType.MESH)

    normed, rstd = rows_norm(hidden_ref[...].astype(f32))
    conv_in = (normed * gain_ref[...]).astype(bf)
    edge[0] = conv_in[BLOCK - 16 :, :]
    edge[1] = conv_in[:16, :]
    pl.semaphore_wait(barrier, 15)
    halo = [
        remote(edge.at[0], far.at[0], e_send.at[0], e_recv.at[0], right),
        remote(edge.at[1], far.at[1], e_send.at[1], e_recv.at[1], left),
    ]
    for l in range(12):
        hhat[l] = normed[:, l * 128 : l * 128 + 128]
        ci[l, 16:144, :] = conv_in[:, l * 128 : l * 128 + 128].astype(f32)
    sums[480:512, :] = jnp.zeros((32, 128), f32)
    wp_load.wait()
    grads = matmul(cot_ref[...], wp[...], 1, 1)
    for l in range(12):
        back[l] = grads[:, l * 128 : l * 128 + 128]

    def place_halo(ref, slot):
        low = jnp.where(s > 0, far[slot].astype(f32), 0.0)
        high = jnp.where(s < 63, far[slot + 1].astype(f32), 0.0)
        for l in range(12):
            ref[l, 0:16, :] = low[:, l * 128 : l * 128 + 128]
            ref[l, 144:160, :] = high[:, l * 128 : l * 128 + 128]

    for copy in halo:
        copy.wait_recv()
    place_halo(ci, 0)

    def forward(l, carry):
        conv = jnp.zeros((BLOCK, 128), f32)
        for j in range(KER):
            conv += taps_ref[l, j : j + 1, :] * ci[l, j : j + BLOCK, :]
        sig = 1.0 / (1.0 + jnp.exp(-conv))
        rounded = (conv * sig).astype(bf)
        lanes = pl.ds(pl.multiple_of(l * 128, 128), 128)
        act[:, lanes] = rounded
        act_t[lanes, :] = rounded.astype(f32).T
        grad = back[l] * (sig * (1.0 + conv * (1.0 - sig)))
        dz[l, 16:144, :] = grad
        for j0 in range(0, KER, 8):
            rows = [
                jnp.sum(grad * ci[l, j : j + BLOCK, :], axis=0, keepdims=True)
                for j in range(j0, j0 + 8)
            ]
            sums[pl.ds(pl.multiple_of(l * 40 + j0, 8), 8), :] = jnp.concatenate(rows, axis=0)
        return carry

    lax.fori_loop(0, 12, forward, 0)
    for l in range(12):
        edge[2, :, l * 128 : l * 128 + 128] = dz[l, 128:144, :].astype(bf)
        edge[3, :, l * 128 : l * 128 + 128] = dz[l, 16:32, :].astype(bf)
    halo = [
        remote(edge.at[2], far.at[2], e_send.at[2], e_recv.at[2], right),
        remote(edge.at[3], far.at[3], e_send.at[3], e_recv.at[3], left),
    ]
    for i in range(8):
        pieces = [act_t[24 * (8 * b + i) : 24 * (8 * b + i) + 24, :] for b in range(8)]
        act_out[i] = jnp.concatenate(pieces, axis=0).astype(bf)
    own_lanes = pl.ds(pl.multiple_of(p * 128, 128), 128)
    act_copies = [
        remote(act_out.at[(p + k) % 8], act_in.at[:, own_lanes],
               a_send.at[k - 1], a_recv.at[k - 1], group[k - 1])
        for k in range(1, 8)
    ]
    act_self = pltpu.make_async_copy(act_out.at[p], act_in.at[:, own_lanes], lsem.at[2])
    act_self.start()
    out_ref[...] = (hidden_ref[...].astype(f32) + matmul(act[...], wp[...])).astype(bf)

    for copy in halo:
        copy.wait_recv()
    place_halo(dz, 2)
    part[...] = jnp.zeros_like(part)

    def backward(l, carry):
        grad = jnp.zeros((BLOCK, 128), f32)
        for j in range(KER):
            grad += taps_ref[l, j : j + 1, :] * dz[l, 32 - j : 32 - j + BLOCK, :]
        row = jnp.sum(grad * hhat[l], axis=0, keepdims=True)
        sums[pl.ds(pl.multiple_of(l * 40 + 32, 8), 8), :] = jnp.concatenate(
            [row, jnp.zeros((7, 128), f32)], axis=0
        )
        lanes = pl.ds(pl.multiple_of(l * 128, 128), 128)
        g = grad * gain_ref[:, lanes]
        back[l] = g
        part[0] += g
        part[1] += g * hhat[l]
        return carry

    lax.fori_loop(0, 12, backward, 0)
    b_copies = [
        remote(sums.at[pl.ds(pl.multiple_of((p + k) % 8 * 64, 64), 64)], b_in.at[k - 1],
               b_send.at[k - 1], b_recv.at[k - 1], group[k - 1])
        for k in range(1, 8)
    ]

    for copy in act_copies:
        copy.wait_recv()
    act_self.wait()
    cots_load.wait()
    tile = matmul(act_in[...], cots[...])
    for b in range(4):
        tile_out[b] = tile[48 * b : 48 * b + 48, :].astype(bf)
    t_copies = [
        remote(tile_out.at[(z + k) % 4], tile_in.at[k - 1],
               t_send.at[k - 1], t_recv.at[k - 1], z_peers[k - 1])
        for k in range(1, 4)
    ]
    for copy in b_copies:
        copy.wait_recv()
    own = pl.ds(pl.multiple_of(p * 64, 64), 64)
    c_in[z] = sums[own, :] + sum(b_in[k] for k in range(7))
    c_copies = [
        remote(c_in.at[z], c_in.at[z], c_send.at[k], c_recv.at[k], z_peers[k]) for k in range(3)
    ]

    mean_g = jnp.sum(part[0], axis=-1, keepdims=True) * (1.0 / D)
    mean_gh = jnp.sum(part[1], axis=-1, keepdims=True) * (1.0 / D)
    for l in range(12):
        lanes = slice(l * 128, l * 128 + 128)
        inner = back[l] - mean_g - hhat[l] * mean_gh
        gh_ref[:, lanes] = (cot_ref[:, lanes].astype(f32) + rstd * inner).astype(bf)

    for copy in c_copies:
        copy.wait_recv()
    d_in[y] = c_in[0] + c_in[1] + c_in[2] + c_in[3]
    d_copies = [
        remote(d_in.at[y], d_in.at[y], d_send.at[k], d_recv.at[k], y_peers[k]) for k in range(3)
    ]
    for copy in t_copies:
        copy.wait_recv()
    mixed = tile_out[z].astype(f32) + sum(tile_in[k].astype(f32) for k in range(3))
    for b in range(2):
        y_out[b] = jnp.concatenate(
            [mixed[24 * b : 24 * b + 24, : D // 2], mixed[24 * b : 24 * b + 24, D // 2 :]], axis=0
        ).astype(bf)
    yt_copies = [
        remote(y_out.at[(y + k) % 4 // 2], y_in.at[y], y_send.at[k - 1], y_recv.at[k - 1],
               y_peers[k - 1])
        for k in range(1, 4)
    ]
    y_in[y] = y_out[y_hi]
    for copy in d_copies:
        copy.wait_recv()
    total[own, :] = d_in[0] + d_in[1] + d_in[2] + d_in[3]
    g_copies = [
        remote(total.at[own], total.at[own], g_send.at[k], g_recv.at[k], group[k])
        for k in range(7)
    ]
    scale = 1.0 / math.sqrt(2 * 64 * BLOCK)
    for copy in yt_copies:
        copy.wait_recv()
    whole = sum(y_in[k].astype(f32) for k in range(4)) * scale
    gp_ref[:, : D // 2] = whole[:24, :]
    gp_ref[:, D // 2 :] = whole[24:, :]
    for copy in g_copies:
        copy.wait_recv()
    for l in range(12):
        lanes = slice(l * 128, l * 128 + 128)
        gk_ref[:, lanes] = total[l * 40 : l * 40 + 32, :] * scale
        gg_ref[:, lanes] = total[l * 40 + 32 : l * 40 + 33, :] * scale
    for copy in copies:
        copy.wait_send()


def conv_module(hidden, gain, taps, w_point, cot, cots):
    bf, f32 = jnp.bfloat16, jnp.float32
    vmem = pl.BlockSpec(memory_space=pltpu.VMEM)
    hbm = pl.BlockSpec(memory_space=pl.ANY)
    dma = pltpu.SemaphoreType.DMA
    shapes = [((BLOCK, D), bf), ((BLOCK, D), bf), ((24, D), f32), ((KER, D), f32), ((1, D), f32)]
    return pl.pallas_call(
        conv_kernel,
        name="conv_module",
        out_shape=tuple(jax.ShapeDtypeStruct(*shape) for shape in shapes),
        in_specs=[vmem, vmem, vmem, hbm, vmem, hbm],
        out_specs=(vmem,) * 5,
        scratch_shapes=[
            pltpu.VMEM((D, D), bf),
            pltpu.VMEM((8 * BLOCK, D), bf),
            pltpu.VMEM((12, BLOCK, 128), f32),
            pltpu.VMEM((12, 160, 128), f32),
            pltpu.VMEM((12, BLOCK, 128), f32),
            pltpu.VMEM((12, 160, 128), f32),
            pltpu.VMEM((BLOCK, D), bf),
            pltpu.VMEM((D, BLOCK), f32),
            pltpu.VMEM((8, 192, 128), bf),
            pltpu.VMEM((192, 1024), bf),
            pltpu.VMEM((4, 16, D), bf),
            pltpu.VMEM((4, 16, D), bf),
            pltpu.VMEM((4, 48, D), bf),
            pltpu.VMEM((3, 48, D), bf),
            pltpu.VMEM((2, 48, D // 2), bf),
            pltpu.VMEM((4, 48, D // 2), bf),
            pltpu.VMEM((2, BLOCK, 128), f32),
            pltpu.VMEM((512, 128), f32),
            pltpu.VMEM((7, 64, 128), f32),
            pltpu.VMEM((4, 64, 128), f32),
            pltpu.VMEM((4, 64, 128), f32),
            pltpu.VMEM((512, 128), f32),
            dma((3,)), dma((4,)), dma((4,)), dma((7,)), dma((7,)), dma((7,)), dma((7,)),
            dma((3,)), dma((3,)), dma((3,)), dma((3,)), dma((7,)), dma((7,)),
            dma((3,)), dma((3,)), dma((3,)), dma((3,)),
        ],
        compiler_params=pltpu.CompilerParams(
            collective_id=1, has_side_effects=True, vmem_limit_bytes=60 << 20
        ),
        cost_estimate=pl.CostEstimate(
            flops=3 * 10**9, bytes_accessed=10 * 2**20, transcendentals=2**18
        ),
    )(hidden, gain, taps, w_point, cot, cots)


def on_device(
    inputs,
    attention_norm_gain,
    w_query,
    w_key,
    w_value,
    w_out,
    gain_conv,
    kernel,
    w_point,
    cotangent,
):
    hidden, cots = attention(
        inputs[0], attention_norm_gain[None], w_key, w_value, w_query, w_out, cotangent[0]
    )
    taps = kernel.reshape(KER, D // 128, 128).transpose(1, 0, 2)
    layer_out, grad_hidden, grad_point, grad_kernel, grad_gain = conv_module(
        hidden, gain_conv[None], taps, w_point, cotangent[0], cots
    )
    return layer_out[None], grad_hidden[None], grad_point, grad_kernel, grad_gain[0]


def solution(mesh):
    placed = (P("utt", "seq", None), P(), P(), P(), P(), P(), P(), P(), P(), P("utt", "seq", None))
    return jax.shard_map(
        on_device,
        mesh=mesh,
        in_specs=placed,
        out_specs=(P("utt", "seq", None), P("utt", "seq", None), P("seq", None), P(), P()),
        check_vma=False,
    )
```

```python
import math

import jax
import jax.numpy as jnp
from jax import lax
from jax.experimental import pallas as pl
from jax.experimental.pallas import tpu as pltpu
from jax.sharding import PartitionSpec as P

D = 1536
HEADS = 8
HEAD_DIM = 96
WIDE = HEADS * HEAD_DIM
KER = 32
BLOCK = 128
HALF = 512
LOG2E = 1.4426950408889634

OWN, SIB, ZM, ZP, Z2, SIB_ZM, SIB_ZP, SIB_Z2 = range(8)


def rows_norm(values):
    mean = jnp.mean(values, axis=-1, keepdims=True)
    centered = values - mean
    rstd = lax.rsqrt(jnp.mean(centered * centered, axis=-1, keepdims=True) + 1e-05)
    return centered * rstd, rstd


def matmul(a, b, da=1, db=0):
    return lax.dot_general(a, b, (((da,), (db,)), ((), ())), preferred_element_type=jnp.float32)


def attention_kernel(
    x_ref, gain_ref, wk_hbm, wv_hbm, wq_hbm, wo_hbm, cot_hbm,
    hidden_ref, cots_hbm,
    wk, wv, wq, wo, normed, kv_out, q_out, kv, qt, acc, top, mix_out, mixt,
    wsem, kv_send, kv_recv, q_send, q_recv, m_send, m_recv, r_send, r_recv, c_send, c_recv,
):
    s = lax.axis_index("seq")
    z = s // 16
    h = (s % 16) // 2
    c = s % 2

    def dev(zz, hh, cc):
        return {"seq": zz * 16 + hh * 2 + cc}

    peers = [dev(z, (h + k) % 8, c) for k in range(1, 8)]
    up, down = dev((z + 1) % 4, h, c), dev((z + 3) % 4, h, c)
    sibling = dev(z, h, 1 - c)

    def remote(src, dst, send, recv, to):
        copy = pltpu.make_async_remote_copy(
            src_ref=src, dst_ref=dst, send_sem=send, recv_sem=recv,
            device_id=to, device_id_type=pl.DeviceIdType.MESH,
        )
        copy.start()
        return copy

    loads = [
        pltpu.make_async_copy(src, dst, wsem.at[i])
        for i, (src, dst) in enumerate(((wk_hbm, wk), (wv_hbm, wv), (wq_hbm, wq), (wo_hbm, wo)))
    ]
    for load in loads:
        load.start()
    for slot in range(16):
        kv[slot, 192:208, :] = jnp.ones((16, HALF), jnp.bfloat16)

    barrier = pltpu.get_barrier_semaphore()
    for to in peers + [up, down, sibling]:
        pl.semaphore_signal(barrier, inc=1, device_id=to, device_id_type=pl.DeviceIdType.MESH)

    xhat, unused_item = rows_norm(x_ref[...].astype(jnp.float32))
    normed[...] = (xhat * gain_ref[...]).astype(jnp.bfloat16)
    loads[0].wait()
    k_rows = matmul(normed[...], wk[...]).T.astype(jnp.bfloat16)
    for i in range(HEADS):
        kv_out[i, 0:96, :] = k_rows[i * 96 : i * 96 + 96, :]
    loads[1].wait()
    v_rows = matmul(normed[...], wv[...]).T.astype(jnp.bfloat16)
    for i in range(HEADS):
        kv_out[i, 96:192, :] = v_rows[i * 96 : i * 96 + 96, :]

    pl.semaphore_wait(barrier, 10)
    mine = pl.ds(pl.multiple_of((h % 4) * 128, 128), 128)
    kv_copies = [
        remote(kv_out.at[(h + k) % 8], kv.at[h // 4, 0:192, mine],
               kv_send.at[k - 1], kv_recv.at[k - 1], peers[k - 1])
        for k in range(1, 8)
    ]
    kv[h // 4, 0:192, mine] = kv_out[h]

    loads[2].wait()
    scale = LOG2E / math.sqrt(HEAD_DIM)
    q_rows = (matmul(normed[...], wq[...]) * scale).T.astype(jnp.bfloat16)
    for i in range(HEADS):
        q_out[i] = q_rows[i * 96 : i * 96 + 96, :]
    lanes = pl.ds(pl.multiple_of(h * 128, 128), 128)
    q_copies = [
        remote(q_out.at[(h + k) % 8], qt.at[:, lanes],
               q_send.at[k - 1], q_recv.at[k - 1], peers[k - 1])
        for k in range(1, 8)
    ]
    qt[:, lanes] = q_out[h]

    sent = []

    def forward(slot, half, to, to_slot):
        sem = len(sent)
        copy = remote(kv.at[2 * slot + half, 0:192], kv.at[2 * to_slot + half, 0:192],
                      r_send.at[sem], r_recv.at[sem], to)
        sent.append(copy)
        return copy

    acc[...] = jnp.zeros_like(acc)
    top[...] = jnp.full_like(top, -1e30)

    def attend(*halves):
        halves = [2 * slot + half for slot, half in halves]
        scores = [matmul(kv[i, 0:96, :], qt[...], 0, 0) for i in halves]
        before = top[0:1, :]
        newest = before
        for part in scores:
            newest = jnp.maximum(newest, jnp.max(part, axis=0, keepdims=True))
        total = acc[...] * jnp.exp2(before - newest)
        for i, part in zip(halves, scores):
            total += matmul(kv[i, 96:208, :], jnp.exp2(part - newest).astype(jnp.bfloat16))
        acc[...] = total
        top[0:1, :] = newest

    for copy in kv_copies:
        copy.wait_recv()
    zm0 = forward(OWN, 0, up, ZM)
    zp1 = forward(OWN, 1, down, ZP)
    sib0 = forward(OWN, 0, sibling, SIB)
    sib1 = forward(OWN, 1, sibling, SIB)
    zm1 = forward(OWN, 1, up, ZM)
    zp0 = forward(OWN, 0, down, ZP)
    x, side = h % 4, h // 4
    own_rows = pl.ds(pl.multiple_of((x * 2 + c) * BLOCK, BLOCK), BLOCK)
    c_copies = [
        remote(cot_hbm, cots_hbm.at[own_rows], c_send.at[k - 1], c_recv.at[k - 1],
               dev(z, side * 4 + (x + k) % 4, c))
        for k in range(1, 4)
    ]
    c_copies.append(
        remote(cot_hbm, cots_hbm.at[own_rows], c_send.at[3], c_recv.at[3], sibling)
    )
    for copy in q_copies:
        copy.wait_recv()
    attend((OWN, 0), (OWN, 1))
    zm0.wait_recv()
    z20 = forward(ZM, 0, up, Z2)
    szm0 = forward(ZM, 0, sibling, SIB_ZM)
    zp1.wait_recv()
    z21 = forward(ZP, 1, down, Z2)
    szp1 = forward(ZP, 1, sibling, SIB_ZP)
    sib0.wait_recv()
    sib1.wait_recv()
    attend((SIB, 0), (SIB, 1), (ZM, 0), (ZP, 1))
    zm1.wait_recv()
    szm1 = forward(ZM, 1, sibling, SIB_ZM)
    zp0.wait_recv()
    szp0 = forward(ZP, 0, sibling, SIB_ZP)
    szm0.wait_recv()
    szp1.wait_recv()
    attend((SIB_ZM, 0), (SIB_ZP, 1), (ZM, 1), (ZP, 0))
    z20.wait_recv()
    sz20 = forward(Z2, 0, sibling, SIB_Z2)
    z21.wait_recv()
    sz21 = forward(Z2, 1, sibling, SIB_Z2)
    szm1.wait_recv()
    szp0.wait_recv()
    for k in range(1, 4):
        c_copies[k - 1].wait_recv()
        rows = pl.ds(pl.multiple_of(((x + 4 - k) % 4 * 2 + c) * BLOCK, BLOCK), BLOCK)
        c_copies.append(
            remote(cots_hbm.at[rows], cots_hbm.at[rows], c_send.at[3 + k], c_recv.at[3 + k], sibling)
        )
    attend((SIB_ZM, 1), (SIB_ZP, 0), (Z2, 0), (Z2, 1))
    sz20.wait_recv()
    sz21.wait_recv()
    attend((SIB_Z2, 0), (SIB_Z2, 1))

    mix_out[...] = (acc[0:96, :] / acc[96:97, :]).astype(jnp.bfloat16)
    band = pl.ds(pl.multiple_of(h * 96, 96), 96)
    m_copies = []
    for k in range(1, 8):
        to_lanes = pl.ds(pl.multiple_of(((h + k) % 8) * 128, 128), 128)
        m_copies.append(
            remote(mix_out.at[:, to_lanes], mixt.at[band, :],
                   m_send.at[k - 1], m_recv.at[k - 1], peers[k - 1])
        )
    mixt[band, :] = mix_out[:, lanes]
    loads[3].wait()
    for copy in m_copies:
        copy.wait_recv()
    hidden_ref[...] = (x_ref[...].astype(jnp.float32) + matmul(mixt[...], wo[...], 0, 0)).astype(
        jnp.bfloat16
    )
    for copy in c_copies[3:]:
        copy.wait_recv()
    for copy in kv_copies + q_copies + sent + m_copies + c_copies:
        copy.wait_send()


def attention(x, gain, w_key, w_value, w_query, w_out, cot):
    bf = jnp.bfloat16
    vmem = pl.BlockSpec(memory_space=pltpu.VMEM)
    hbm = pl.BlockSpec(memory_space=pl.ANY)
    dma = pltpu.SemaphoreType.DMA
    return pl.pallas_call(
        attention_kernel,
        name="attention",
        out_shape=(jax.ShapeDtypeStruct((BLOCK, D), bf), jax.ShapeDtypeStruct((8 * BLOCK, D), bf)),
        in_specs=[vmem, vmem, hbm, hbm, hbm, hbm, hbm],
        out_specs=(vmem, hbm),
        scratch_shapes=[
            pltpu.VMEM((D, WIDE), bf),
            pltpu.VMEM((D, WIDE), bf),
            pltpu.VMEM((D, WIDE), bf),
            pltpu.VMEM((WIDE, D), bf),
            pltpu.VMEM((BLOCK, D), bf),
            pltpu.VMEM((HEADS, 192, 128), bf),
            pltpu.VMEM((HEADS, 96, 128), bf),
            pltpu.VMEM((16, 208, HALF), bf),
            pltpu.VMEM((96, 1024), bf),
            pltpu.VMEM((112, 1024), jnp.float32),
            pltpu.VMEM((8, 1024), jnp.float32),
            pltpu.VMEM((96, 1024), bf),
            pltpu.VMEM((WIDE, 128), bf),
            dma((4,)), dma((7,)), dma((7,)), dma((7,)), dma((7,)), dma((7,)), dma((7,)),
            dma((14,)), dma((14,)), dma((7,)), dma((7,)),
        ],
        compiler_params=pltpu.CompilerParams(
            collective_id=0, has_side_effects=True, vmem_limit_bytes=60 << 20
        ),
        cost_estimate=pl.CostEstimate(
            flops=6 * 10**9, bytes_accessed=10 * 2**20, transcendentals=2**23
        ),
    )(x, gain, w_key, w_value, w_query, w_out, cot)


def conv_kernel(
    hidden_ref, gain_ref, taps_ref, wp_hbm, cot_ref, cots_hbm,
    out_ref, gh_ref, gp_ref, gk_ref, gg_ref,
    wp, cots, hhat, ci, back, dz, act, act_t, act_out, act_in, edge, far, tile_out, tile_in,
    y_out, y_in, part, sums, b_in, c_in, d_in, total,
    lsem, e_send, e_recv, a_send, a_recv, b_send, b_recv, c_send, c_recv, d_send, d_recv,
    g_send, g_recv, t_send, t_recv, y_send, y_recv,
):
    f32, bf = jnp.float32, jnp.bfloat16
    s = lax.axis_index("seq")
    u = lax.axis_index("utt")
    z, y_hi, x, c = s // 16, (s // 8) % 2, (s // 2) % 4, s % 2
    p, y = s % 8, y_hi * 2 + u
    right, left = {"seq": (s + 1) % 64}, {"seq": (s + 63) % 64}
    group = [{"seq": s // 8 * 8 + (p + k) % 8} for k in range(1, 8)]
    z_peers = [{"seq": (z + k) % 4 * 16 + s % 16} for k in range(1, 4)]
    y_peers = [
        {"seq": z * 16 + (y + k) % 4 // 2 * 8 + p, "utt": (y + k) % 4 % 2} for k in range(1, 4)
    ]
    copies = []

    def remote(src, dst, send, recv, to):
        copy = pltpu.make_async_remote_copy(
            src_ref=src, dst_ref=dst, send_sem=send, recv_sem=recv,
            device_id=to, device_id_type=pl.DeviceIdType.MESH,
        )
        copy.start()
        copies.append(copy)
        return copy

    wp_load = pltpu.make_async_copy(wp_hbm, wp, lsem.at[0])
    wp_load.start()
    own_rows = pl.ds(pl.multiple_of(p * BLOCK, BLOCK), BLOCK)
    cots_loads = []
    for k in range(1, 8):
        rows = pl.ds(pl.multiple_of((p + k) % 8 * BLOCK, BLOCK), BLOCK)
        cots_loads.append(pltpu.make_async_copy(cots_hbm.at[rows], cots.at[rows], lsem.at[k]))
        cots_loads[-1].start()
    cots[own_rows, :] = cot_ref[...]
    barrier = pltpu.get_barrier_semaphore()
    for to in [right, left] + group + z_peers + y_peers:
        pl.semaphore_signal(barrier, inc=1, device_id=to, device_id_type=pl.DeviceIdType.MESH)

    normed, rstd = rows_norm(hidden_ref[...].astype(f32))
    conv_in = (normed * gain_ref[...]).astype(bf)
    edge[0] = conv_in[BLOCK - 16 :, :]
    edge[1] = conv_in[:16, :]
    pl.semaphore_wait(barrier, 15)
    halo = [
        remote(edge.at[0], far.at[0], e_send.at[0], e_recv.at[0], right),
        remote(edge.at[1], far.at[1], e_send.at[1], e_recv.at[1], left),
    ]
    for l in range(12):
        hhat[l] = normed[:, l * 128 : l * 128 + 128]
        ci[l, 16:144, :] = conv_in[:, l * 128 : l * 128 + 128].astype(f32)
    sums[480:512, :] = jnp.zeros((32, 128), f32)
    wp_load.wait()
    grads = matmul(cot_ref[...], wp[...], 1, 1)
    for l in range(12):
        back[l] = grads[:, l * 128 : l * 128 + 128]

    def place_halo(ref, slot):
        low = jnp.where(s > 0, far[slot].astype(f32), 0.0)
        high = jnp.where(s < 63, far[slot + 1].astype(f32), 0.0)
        for l in range(12):
            ref[l, 0:16, :] = low[:, l * 128 : l * 128 + 128]
            ref[l, 144:160, :] = high[:, l * 128 : l * 128 + 128]

    for copy in halo:
        copy.wait_recv()
    place_halo(ci, 0)

    def forward(l, carry):
        conv = jnp.zeros((BLOCK, 128), f32)
        for j in range(KER):
            conv += taps_ref[l, j : j + 1, :] * ci[l, j : j + BLOCK, :]
        sig = 1.0 / (1.0 + jnp.exp(-conv))
        rounded = (conv * sig).astype(bf)
        lanes = pl.ds(pl.multiple_of(l * 128, 128), 128)
        act[:, lanes] = rounded
        act_t[lanes, :] = rounded.astype(f32).T
        grad = back[l] * (sig * (1.0 + conv * (1.0 - sig)))
        dz[l, 16:144, :] = grad
        for j0 in range(0, KER, 8):
            rows = [
                jnp.sum(grad * ci[l, j : j + BLOCK, :], axis=0, keepdims=True)
                for j in range(j0, j0 + 8)
            ]
            sums[pl.ds(pl.multiple_of(l * 40 + j0, 8), 8), :] = jnp.concatenate(rows, axis=0)
        return carry

    lax.fori_loop(0, 12, forward, 0)
    for l in range(12):
        edge[2, :, l * 128 : l * 128 + 128] = dz[l, 128:144, :].astype(bf)
        edge[3, :, l * 128 : l * 128 + 128] = dz[l, 16:32, :].astype(bf)
    halo = [
        remote(edge.at[2], far.at[2], e_send.at[2], e_recv.at[2], right),
        remote(edge.at[3], far.at[3], e_send.at[3], e_recv.at[3], left),
    ]
    for i in range(8):
        pieces = [act_t[24 * (8 * b + i) : 24 * (8 * b + i) + 24, :] for b in range(8)]
        act_out[i] = jnp.concatenate(pieces, axis=0).astype(bf)
    own_lanes = pl.ds(pl.multiple_of(p * 128, 128), 128)
    act_copies = [
        remote(act_out.at[(p + k) % 8], act_in.at[:, own_lanes],
               a_send.at[k - 1], a_recv.at[k - 1], group[k - 1])
        for k in range(1, 8)
    ]
    act_in[:, own_lanes] = act_out[p]
    out_ref[...] = (hidden_ref[...].astype(f32) + matmul(act[...], wp[...])).astype(bf)

    for copy in halo:
        copy.wait_recv()
    place_halo(dz, 2)
    part[...] = jnp.zeros_like(part)

    def backward(l, carry):
        grad = jnp.zeros((BLOCK, 128), f32)
        for j in range(KER):
            grad += taps_ref[l, j : j + 1, :] * dz[l, 32 - j : 32 - j + BLOCK, :]
        row = jnp.sum(grad * hhat[l], axis=0, keepdims=True)
        sums[pl.ds(pl.multiple_of(l * 40 + 32, 8), 8), :] = jnp.concatenate(
            [row, jnp.zeros((7, 128), f32)], axis=0
        )
        lanes = pl.ds(pl.multiple_of(l * 128, 128), 128)
        g = grad * gain_ref[:, lanes]
        back[l] = g
        part[0] += g
        part[1] += g * hhat[l]
        return carry

    lax.fori_loop(0, 12, backward, 0)
    b_copies = [
        remote(sums.at[pl.ds(pl.multiple_of((p + k) % 8 * 64, 64), 64)], b_in.at[k - 1],
               b_send.at[k - 1], b_recv.at[k - 1], group[k - 1])
        for k in range(1, 8)
    ]

    for copy in act_copies:
        copy.wait_recv()
    for load in cots_loads:
        load.wait()
    tile = matmul(act_in[...], cots[...])
    for b in range(4):
        tile_out[b] = tile[48 * b : 48 * b + 48, :].astype(bf)
    t_copies = [
        remote(tile_out.at[(z + k) % 4], tile_in.at[k - 1],
               t_send.at[k - 1], t_recv.at[k - 1], z_peers[k - 1])
        for k in range(1, 4)
    ]
    for copy in b_copies:
        copy.wait_recv()
    own = pl.ds(pl.multiple_of(p * 64, 64), 64)
    c_in[z] = sums[own, :] + sum(b_in[k] for k in range(7))
    c_copies = [
        remote(c_in.at[z], c_in.at[z], c_send.at[k], c_recv.at[k], z_peers[k]) for k in range(3)
    ]

    mean_g = jnp.sum(part[0], axis=-1, keepdims=True) * (1.0 / D)
    mean_gh = jnp.sum(part[1], axis=-1, keepdims=True) * (1.0 / D)
    for l in range(12):
        lanes = slice(l * 128, l * 128 + 128)
        inner = back[l] - mean_g - hhat[l] * mean_gh
        gh_ref[:, lanes] = (cot_ref[:, lanes].astype(f32) + rstd * inner).astype(bf)

    for copy in c_copies:
        copy.wait_recv()
    d_in[y] = c_in[0] + c_in[1] + c_in[2] + c_in[3]
    d_copies = [
        remote(d_in.at[y], d_in.at[y], d_send.at[k], d_recv.at[k], y_peers[k]) for k in range(3)
    ]
    for copy in t_copies:
        copy.wait_recv()
    mixed = tile_out[z].astype(f32) + sum(tile_in[k].astype(f32) for k in range(3))
    for b in range(2):
        y_out[b] = jnp.concatenate(
            [mixed[24 * b : 24 * b + 24, : D // 2], mixed[24 * b : 24 * b + 24, D // 2 :]], axis=0
        ).astype(bf)
    yt_copies = [
        remote(y_out.at[(y + k) % 4 // 2], y_in.at[y], y_send.at[k - 1], y_recv.at[k - 1],
               y_peers[k - 1])
        for k in range(1, 4)
    ]
    y_in[y] = y_out[y_hi]
    for copy in d_copies:
        copy.wait_recv()
    total[own, :] = d_in[0] + d_in[1] + d_in[2] + d_in[3]
    g_copies = [
        remote(total.at[own], total.at[own], g_send.at[k], g_recv.at[k], group[k])
        for k in range(7)
    ]
    scale = 1.0 / math.sqrt(2 * 64 * BLOCK)
    for copy in yt_copies:
        copy.wait_recv()
    whole = sum(y_in[k].astype(f32) for k in range(4)) * scale
    gp_ref[:, : D // 2] = whole[:24, :]
    gp_ref[:, D // 2 :] = whole[24:, :]
    for copy in g_copies:
        copy.wait_recv()
    for l in range(12):
        lanes = slice(l * 128, l * 128 + 128)
        gk_ref[:, lanes] = total[l * 40 : l * 40 + 32, :] * scale
        gg_ref[:, lanes] = total[l * 40 + 32 : l * 40 + 33, :] * scale
    for copy in copies:
        copy.wait_send()


def conv_module(hidden, gain, taps, w_point, cot, cots):
    bf, f32 = jnp.bfloat16, jnp.float32
    vmem = pl.BlockSpec(memory_space=pltpu.VMEM)
    hbm = pl.BlockSpec(memory_space=pl.ANY)
    dma = pltpu.SemaphoreType.DMA
    shapes = [((BLOCK, D), bf), ((BLOCK, D), bf), ((24, D), f32), ((KER, D), f32), ((1, D), f32)]
    return pl.pallas_call(
        conv_kernel,
        name="conv_module",
        out_shape=tuple(jax.ShapeDtypeStruct(*shape) for shape in shapes),
        in_specs=[vmem, vmem, vmem, hbm, vmem, hbm],
        out_specs=(vmem,) * 5,
        scratch_shapes=[
            pltpu.VMEM((D, D), bf),
            pltpu.VMEM((8 * BLOCK, D), bf),
            pltpu.VMEM((12, BLOCK, 128), f32),
            pltpu.VMEM((12, 160, 128), f32),
            pltpu.VMEM((12, BLOCK, 128), f32),
            pltpu.VMEM((12, 160, 128), f32),
            pltpu.VMEM((BLOCK, D), bf),
            pltpu.VMEM((D, BLOCK), f32),
            pltpu.VMEM((8, 192, 128), bf),
            pltpu.VMEM((192, 1024), bf),
            pltpu.VMEM((4, 16, D), bf),
            pltpu.VMEM((4, 16, D), bf),
            pltpu.VMEM((4, 48, D), bf),
            pltpu.VMEM((3, 48, D), bf),
            pltpu.VMEM((2, 48, D // 2), bf),
            pltpu.VMEM((4, 48, D // 2), bf),
            pltpu.VMEM((2, BLOCK, 128), f32),
            pltpu.VMEM((512, 128), f32),
            pltpu.VMEM((7, 64, 128), f32),
            pltpu.VMEM((4, 64, 128), f32),
            pltpu.VMEM((4, 64, 128), f32),
            pltpu.VMEM((512, 128), f32),
            dma((8,)), dma((4,)), dma((4,)), dma((7,)), dma((7,)), dma((7,)), dma((7,)),
            dma((3,)), dma((3,)), dma((3,)), dma((3,)), dma((7,)), dma((7,)),
            dma((3,)), dma((3,)), dma((3,)), dma((3,)),
        ],
        compiler_params=pltpu.CompilerParams(
            collective_id=1, has_side_effects=True, vmem_limit_bytes=60 << 20
        ),
        cost_estimate=pl.CostEstimate(
            flops=3 * 10**9, bytes_accessed=10 * 2**20, transcendentals=2**18
        ),
    )(hidden, gain, taps, w_point, cot, cots)


def on_device(
    inputs,
    attention_norm_gain,
    w_query,
    w_key,
    w_value,
    w_out,
    gain_conv,
    kernel,
    w_point,
    cotangent,
):
    hidden, cots = attention(
        inputs[0], attention_norm_gain[None], w_key, w_value, w_query, w_out, cotangent[0]
    )
    taps = kernel.reshape(KER, D // 128, 128).transpose(1, 0, 2)
    layer_out, grad_hidden, grad_point, grad_kernel, grad_gain = conv_module(
        hidden, gain_conv[None], taps, w_point, cotangent[0], cots
    )
    return layer_out[None], grad_hidden[None], grad_point, grad_kernel, grad_gain[0]


def solution(mesh):
    placed = (P("utt", "seq", None), P(), P(), P(), P(), P(), P(), P(), P(), P("utt", "seq", None))
    return jax.shard_map(
        on_device,
        mesh=mesh,
        in_specs=placed,
        out_specs=(P("utt", "seq", None), P("utt", "seq", None), P("seq", None), P(), P()),
        check_vma=False,
    )
```

```python
import math

import jax
import jax.numpy as jnp
from jax import lax
from jax.experimental import pallas as pl
from jax.experimental.pallas import tpu as pltpu
from jax.sharding import PartitionSpec as P

D = 1536
HEADS = 8
HEAD_DIM = 96
WIDE = HEADS * HEAD_DIM
KER = 32
BLOCK = 128
HALF = 512
LOG2E = 1.4426950408889634

OWN, SIB, ZM, ZP, Z2, SIB_ZM, SIB_ZP, SIB_Z2 = range(8)


def rows_norm(values):
    mean = jnp.mean(values, axis=-1, keepdims=True)
    centered = values - mean
    rstd = lax.rsqrt(jnp.mean(centered * centered, axis=-1, keepdims=True) + 1e-05)
    return centered * rstd, rstd


def matmul(a, b, da=1, db=0):
    return lax.dot_general(a, b, (((da,), (db,)), ((), ())), preferred_element_type=jnp.float32)


def layer_kernel(
    x_ref, gain_ref, wk_hbm, wv_hbm, wq_hbm, wo_hbm, gain_conv_ref, taps_ref, wp_hbm, cot_ref,
    out_ref, gh_ref, gp_ref, gk_ref, gg_ref,
    wk, wv, wq, wo, wp, normed, kv_out, q_out, kv, qt, acc, top, mix_out, mixt, cots,
    hidden, hhat, ci, back, dz, conv, act, act_t, act_out, act_in, edge, halo, tile_out, tile_in,
    y_out, y_in, part, sums, b_out, b_in, c_in, d_in, total,
    w_sem, kv_send, kv_recv, q_send, q_recv, m_send, m_recv, r_send, r_recv, s_send, s_recv,
    e_send, e_recv, a_send, a_recv, b_send, b_recv, c_send, c_recv, d_send, d_recv,
    g_send, g_recv, t_send, t_recv, y_send, y_recv,
):
    f32, bf = jnp.float32, jnp.bfloat16
    s = lax.axis_index("seq")
    u = lax.axis_index("utt")
    z, y_hi, x, c = s // 16, (s // 8) % 2, (s // 2) % 4, s % 2
    h, p, y = y_hi * 4 + x, s % 8, y_hi * 2 + u

    def dev(zz, hh, cc):
        return {"seq": zz * 16 + hh * 2 + cc}

    def plane(side, step, sign=1):
        return (y_hi + side) % 2 * 4 + (x + sign * step + 4) % 4

    near = [(0, 1), (0, 2), (0, 3)]
    away = [(1, 0), (1, 1), (1, 2), (1, 3)]
    up, down, sibling = dev((z + 1) % 4, h, c), dev((z + 3) % 4, h, c), dev(z, h, 1 - c)
    right, left = {"seq": (s + 1) % 64}, {"seq": (s + 63) % 64}
    group = [{"seq": s // 8 * 8 + (p + k) % 8} for k in range(1, 8)]
    z_peers = [dev((z + k) % 4, h, c) for k in range(1, 4)]
    y_peers = [
        {"seq": z * 16 + (y + k) % 4 // 2 * 8 + p, "utt": (y + k) % 4 % 2} for k in range(1, 4)
    ]
    copies = []

    def remote(src, dst, send, recv, to):
        copy = pltpu.make_async_remote_copy(
            src_ref=src, dst_ref=dst, send_sem=send, recv_sem=recv,
            device_id=to, device_id_type=pl.DeviceIdType.MESH,
        )
        copy.start()
        copies.append(copy)
        return copy

    def arrive(group_of_copies):
        for copy in group_of_copies:
            copy.wait_recv()

    loads = {}
    sem = 0
    for name, src, dst, cuts in (
        ("k", wk_hbm, wk, 2), ("v", wv_hbm, wv, 2), ("q", wq_hbm, wq, 2),
        ("p", wp_hbm, wp, 2), ("o", wo_hbm, wo, 2),
    ):
        rows = dst.shape[0] // cuts
        loads[name] = []
        for i in range(cuts):
            cut = pl.ds(i * rows, rows)
            loads[name].append(pltpu.make_async_copy(src.at[cut], dst.at[cut], w_sem.at[sem]))
            loads[name][-1].start()
            sem += 1

    def loaded(name):
        for load in loads[name]:
            load.wait()

    for slot in range(16):
        kv[slot, 192:208, :] = jnp.ones((16, HALF), bf)
    barrier = pltpu.get_barrier_semaphore()
    greeted = [dev(z, plane(a, b), c) for a, b in near + away] + group + z_peers + y_peers
    greeted += [right, left]
    for to in greeted:
        pl.semaphore_signal(barrier, inc=1, device_id=to, device_id_type=pl.DeviceIdType.MESH)

    xhat, unused_item = rows_norm(x_ref[...].astype(f32))
    normed[...] = (xhat * gain_ref[...].reshape(1, D)).astype(bf)
    loaded("k")
    rows = matmul(normed[...], wk[...]).T.astype(bf)
    for i in range(HEADS):
        kv_out[i, 0:96, :] = rows[i * 96 : i * 96 + 96, :]
    loaded("v")
    rows = matmul(normed[...], wv[...]).T.astype(bf)
    for i in range(HEADS):
        kv_out[i, 96:192, :] = rows[i * 96 : i * 96 + 96, :]
    pl.semaphore_wait(barrier, len(greeted))
    mine = pl.ds(pl.multiple_of(x * 128, 128), 128)
    lanes = pl.ds(pl.multiple_of(h * 128, 128), 128)

    def exchange(src, dst, send, recv, peers):
        made = []
        for a, b in peers:
            to = plane(a, b)
            made.append(remote(src(to), dst, send.at[4 * a + b], recv.at[4 * a + b], dev(z, to, c)))
        return made

    kv_near = exchange(lambda i: kv_out.at[i], kv.at[y_hi, 0:192, mine], kv_send, kv_recv, near)
    kv_away = exchange(lambda i: kv_out.at[i], kv.at[y_hi, 0:192, mine], kv_send, kv_recv, away)
    kv[y_hi, 0:192, mine] = kv_out[h]
    loaded("q")
    rows = (matmul(normed[...], wq[...]) * (LOG2E / math.sqrt(HEAD_DIM))).T.astype(bf)
    for i in range(HEADS):
        q_out[i] = rows[i * 96 : i * 96 + 96, :]
    q_near = exchange(lambda i: q_out.at[i], qt.at[:, lanes], q_send, q_recv, near)
    q_away = exchange(lambda i: q_out.at[i], qt.at[:, lanes], q_send, q_recv, away)
    qt[:, lanes] = q_out[h]
    acc[...] = jnp.zeros_like(acc)
    top[...] = jnp.full_like(top, -1e30)

    NEAR, AWAY = y_hi, 1 - y_hi
    hops = []

    def forward(slot, half, to, to_slot):
        i = len(hops)
        copy = remote(kv.at[2 * slot + half, 0:192], kv.at[2 * to_slot + half, 0:192],
                      r_send.at[i], r_recv.at[i], to)
        hops.append(copy)
        return copy

    def attend(side, *halves):
        span = pl.ds(pl.multiple_of(side * HALF, HALF), HALF)
        halves = [2 * slot + half for slot, half in halves]
        scores = [matmul(kv[i, 0:96, :], qt[:, span], 0, 0) for i in halves]
        before = top[0:1, span]
        newest = before
        for one in scores:
            newest = jnp.maximum(newest, jnp.max(one, axis=0, keepdims=True))
        result = acc[:, span] * jnp.exp2(before - newest)
        for i, one in zip(halves, scores):
            result += matmul(kv[i, 96:208, :], jnp.exp2(one - newest).astype(bf))
        acc[:, span] = result
        top[0:1, span] = newest

    def attend_both(*halves):
        def one_side(side, carry):
            attend(side, *halves)
            return carry

        lax.fori_loop(0, 2, one_side, 0)

    arrive(kv_near)
    zm_n = forward(OWN, NEAR, up, ZM)
    zp_n = forward(OWN, NEAR, down, ZP)
    sib_n = forward(OWN, NEAR, sibling, SIB)
    loaded("p")
    grads = matmul(cot_ref[...], wp[...], 1, 1)
    for l in range(12):
        back[l] = grads[:, l * 128 : l * 128 + 128]
    arrive(kv_away)
    zp_a = forward(OWN, AWAY, down, ZP)
    zm_a = forward(OWN, AWAY, up, ZM)
    sib_a = forward(OWN, AWAY, sibling, SIB)
    arrive(q_near)
    sib_n.wait_recv()
    attend(NEAR, (OWN, NEAR), (SIB, NEAR))
    arrive(q_away)
    own_rows = pl.ds(pl.multiple_of(p * BLOCK, BLOCK), BLOCK)
    cots[own_rows, :] = cot_ref[...]
    cot_copies = [
        remote(cot_ref, cots.at[own_rows], s_send.at[k], s_recv.at[k], dev(z, plane(0, k), c))
        for k in range(1, 4)
    ]
    cot_copies.append(remote(cot_ref, cots.at[own_rows], s_send.at[0], s_recv.at[0], sibling))
    attend(AWAY, (OWN, NEAR), (SIB, NEAR))
    sib_a.wait_recv()
    attend_both((OWN, AWAY), (SIB, AWAY))
    zm_n.wait_recv()
    z2_n = forward(ZM, NEAR, up, Z2)
    szm_n = forward(ZM, NEAR, sibling, SIB_ZM)
    zp_n.wait_recv()
    szp_n = forward(ZP, NEAR, sibling, SIB_ZP)
    attend_both((ZM, NEAR), (ZP, NEAR))
    zp_a.wait_recv()
    z2_a = forward(ZP, AWAY, down, Z2)
    szp_a = forward(ZP, AWAY, sibling, SIB_ZP)
    zm_a.wait_recv()
    szm_a = forward(ZM, AWAY, sibling, SIB_ZM)
    arrive([szm_n, szp_n])
    attend_both((SIB_ZM, NEAR), (SIB_ZP, NEAR), (ZM, AWAY), (ZP, AWAY))
    z2_n.wait_recv()
    sz2_n = forward(Z2, NEAR, sibling, SIB_Z2)
    z2_a.wait_recv()
    sz2_a = forward(Z2, AWAY, sibling, SIB_Z2)
    arrive([szm_a, szp_a])
    attend_both((SIB_ZM, AWAY), (SIB_ZP, AWAY), (Z2, NEAR), (Z2, AWAY))
    arrive(cot_copies)
    cot_relays = []
    for k in range(1, 4):
        rows = pl.ds(pl.multiple_of((plane(0, k, -1) % 4 * 2 + c) * BLOCK, BLOCK), BLOCK)
        cot_relays.append(
            remote(cots.at[rows], cots.at[rows], s_send.at[3 + k], s_recv.at[3 + k], sibling)
        )
    arrive([sz2_n, sz2_a])
    band = pl.ds(pl.multiple_of(h * 96, 96), 96)

    def give_back(side, peers):
        span = pl.ds(pl.multiple_of(side * HALF, HALF), HALF)
        mix_out[:, span] = (acc[0:96, span] / acc[96:97, span]).astype(bf)
        return exchange(
            lambda i: mix_out.at[:, pl.ds(pl.multiple_of(i * 128, 128), 128)],
            mixt.at[band, :], m_send, m_recv, peers,
        )

    attend(AWAY, (SIB_Z2, NEAR), (SIB_Z2, AWAY))
    m_away = give_back(AWAY, away)
    attend(NEAR, (SIB_Z2, NEAR), (SIB_Z2, AWAY))
    m_near = give_back(NEAR, near)
    mixt[band, :] = mix_out[:, lanes]
    loaded("o")
    arrive(m_away + m_near)
    hidden[...] = (x_ref[...].astype(f32) + matmul(mixt[...], wo[...], 0, 0)).astype(bf)

    standard, rstd = rows_norm(hidden[...].astype(f32))
    conv_in = (standard * gain_conv_ref[...].reshape(1, D)).astype(bf)
    edge[0] = conv_in[BLOCK - 16 :, :]
    edge[1] = conv_in[:16, :]
    halos = [
        remote(edge.at[0], halo.at[0], e_send.at[0], e_recv.at[0], right),
        remote(edge.at[1], halo.at[1], e_send.at[1], e_recv.at[1], left),
    ]
    for l in range(12):
        hhat[l] = standard[:, l * 128 : l * 128 + 128]
        ci[l, 16:144, :] = conv_in[:, l * 128 : l * 128 + 128].astype(f32)
    sums[480:512, :] = jnp.zeros((32, 128), f32)

    def place_halo(ref, slot):
        low = jnp.where(s > 0, halo[slot].astype(f32), 0.0)
        high = jnp.where(s < 63, halo[slot + 1].astype(f32), 0.0)
        for l in range(12):
            ref[l, 0:16, :] = low[:, l * 128 : l * 128 + 128]
            ref[l, 144:160, :] = high[:, l * 128 : l * 128 + 128]

    def span_of(l):
        return pl.ds(pl.multiple_of(l * 128, 128), 128)

    def conv_rows(l, first, count):
        result = jnp.zeros((count, 128), f32)
        for j in range(KER):
            result += taps_ref[j : j + 1, span_of(l)] * ci[l, first + j : first + j + count, :]
        conv[l, first : first + count, :] = result

    def grad_rows(l, first, count):
        result = jnp.zeros((count, 128), f32)
        for j in range(KER):
            start = first + 32 - j
            result += taps_ref[j : j + 1, span_of(l)] * dz[l, start : start + count, :]
        return result

    def middle(l, carry):
        conv_rows(l, 16, 96)
        return carry

    lax.fori_loop(0, 12, middle, 0)
    arrive(halos)
    place_halo(ci, 0)

    def activate(l, carry):
        conv_rows(l, 0, 16)
        conv_rows(l, 112, 16)
        value = conv[l]
        sig = 1.0 / (1.0 + jnp.exp(-value))
        rounded = (value * sig).astype(bf)
        act[:, span_of(l)] = rounded
        act_t[span_of(l), :] = rounded.astype(f32).T
        dz[l, 16:144, :] = back[l] * (sig * (1.0 + value * (1.0 - sig)))
        return carry

    lax.fori_loop(0, 12, activate, 0)
    for l in range(12):
        edge[2, :, l * 128 : l * 128 + 128] = dz[l, 128:144, :].astype(bf)
        edge[3, :, l * 128 : l * 128 + 128] = dz[l, 16:32, :].astype(bf)
    halos = [
        remote(edge.at[2], halo.at[2], e_send.at[2], e_recv.at[2], right),
        remote(edge.at[3], halo.at[3], e_send.at[3], e_recv.at[3], left),
    ]
    for i in range(8):
        pieces = [act_t[24 * (8 * b + i) : 24 * (8 * b + i) + 24, :] for b in range(8)]
        act_out[i] = jnp.concatenate(pieces, axis=0).astype(bf)
    own_lanes = pl.ds(pl.multiple_of(p * 128, 128), 128)
    act_copies = [
        remote(act_out.at[(p + k) % 8], act_in.at[:, own_lanes],
               a_send.at[k - 1], a_recv.at[k - 1], group[k - 1])
        for k in range(1, 8)
    ]
    act_in[:, own_lanes] = act_out[p]

    def taps_grad(l, carry):
        grad = dz[l, 16:144, :]
        for j0 in range(0, KER, 8):
            rows = [
                jnp.sum(grad * ci[l, j : j + BLOCK, :], axis=0, keepdims=True)
                for j in range(j0, j0 + 8)
            ]
            sums[pl.ds(pl.multiple_of(l * 40 + j0, 8), 8), :] = jnp.concatenate(rows, axis=0)
        return carry

    lax.fori_loop(0, 12, taps_grad, 0)

    arrive(halos)
    place_halo(dz, 2)
    part[...] = jnp.zeros_like(part)

    def backward(l, carry):
        grad = grad_rows(l, 0, BLOCK)
        row = jnp.sum(grad * hhat[l], axis=0, keepdims=True)
        sums[pl.ds(pl.multiple_of(l * 40 + 32, 8), 8), :] = jnp.concatenate(
            [row, jnp.zeros((7, 128), f32)], axis=0
        )
        g = grad * gain_conv_ref[span_of(l)].reshape(1, 128)
        back[l] = g
        part[0] += g
        part[1] += g * hhat[l]
        return carry

    lax.fori_loop(0, 12, backward, 0)
    b_out[...] = sums[...].astype(bf)
    b_copies = [
        remote(b_out.at[pl.ds(pl.multiple_of((p + k) % 8 * 64, 64), 64)], b_in.at[k - 1],
               b_send.at[k - 1], b_recv.at[k - 1], group[k - 1])
        for k in range(1, 8)
    ]

    arrive(act_copies)
    arrive(cot_relays)
    t_copies = []
    for i in range(2):
        tile = matmul(act_in[...], cots[:, i * 768 : i * 768 + 768])
        for b in range(4):
            tile_out[i, b] = tile[48 * b : 48 * b + 48, :].astype(bf)
        t_copies.append([
            remote(tile_out.at[i, (z + k) % 4], tile_in.at[i, k - 1],
                   t_send.at[3 * i + k - 1], t_recv.at[3 * i + k - 1], z_peers[k - 1])
            for k in range(1, 4)
        ])
    arrive(b_copies)
    own = pl.ds(pl.multiple_of(p * 64, 64), 64)
    c_in[z] = (sums[own, :] + sum(b_in[k].astype(f32) for k in range(7))).astype(bf)
    c_copies = [
        remote(c_in.at[z], c_in.at[z], c_send.at[k], c_recv.at[k], z_peers[k]) for k in range(3)
    ]
    out_ref[...] = (hidden[...].astype(f32) + matmul(act[...], wp[...])).astype(bf)
    arrive(c_copies)
    d_in[y] = sum(c_in[k].astype(f32) for k in range(4)).astype(bf)
    d_copies = [
        remote(d_in.at[y], d_in.at[y], d_send.at[k], d_recv.at[k], y_peers[k]) for k in range(3)
    ]
    mean_g = jnp.sum(part[0], axis=-1, keepdims=True) * (1.0 / D)
    mean_gh = jnp.sum(part[1], axis=-1, keepdims=True) * (1.0 / D)
    for l in range(12):
        cut = slice(l * 128, l * 128 + 128)
        inner = back[l] - mean_g - hhat[l] * mean_gh
        gh_ref[:, cut] = (cot_ref[:, cut].astype(f32) + rstd * inner).astype(bf)
    y_copies = []

    def along_y(i):
        arrive(t_copies[i])
        mixed = tile_out[i, z].astype(f32) + sum(tile_in[i, k].astype(f32) for k in range(3))
        for b in range(2):
            rows = mixed[24 * b : 24 * b + 24, :]
            y_out[i, b] = jnp.concatenate([rows[:, :384], rows[:, 384:]], axis=0).astype(bf)
        y_copies.append([
            remote(y_out.at[i, (y + k) % 4 // 2], y_in.at[i, y],
                   y_send.at[3 * i + k - 1], y_recv.at[3 * i + k - 1], y_peers[k - 1])
            for k in range(1, 4)
        ])
        y_in[i, y] = y_out[i, y_hi]

    along_y(0)
    arrive(d_copies)
    total[own, :] = sum(d_in[k].astype(f32) for k in range(4)).astype(bf)
    g_copies = [
        remote(total.at[own], total.at[own], g_send.at[k], g_recv.at[k], group[k])
        for k in range(7)
    ]
    along_y(1)
    scale = 1.0 / math.sqrt(2 * 64 * BLOCK)
    for i in range(2):
        arrive(y_copies[i])
        whole = sum(y_in[i, k].astype(f32) for k in range(4)) * scale
        gp_ref[:, i * 768 : i * 768 + 384] = whole[:24, :]
        gp_ref[:, i * 768 + 384 : i * 768 + 768] = whole[24:, :]
    arrive(g_copies)
    for l in range(12):
        cut = slice(l * 128, l * 128 + 128)
        gk_ref[:, cut] = total[l * 40 : l * 40 + 32, :].astype(f32) * scale
        gg_ref[:, cut] = total[l * 40 + 32 : l * 40 + 40, :].astype(f32)[:1, :] * scale
    for copy in copies:
        copy.wait_send()


def finish_kernel(out, gh, gp, gk, gg, out_to, gh_to, gp_to, gk_to, gg_to, sem):
    pairs = ((out, out_to), (gh, gh_to), (gp, gp_to), (gk, gk_to))
    moves = [pltpu.make_async_copy(src, dst, sem.at[i]) for i, (src, dst) in enumerate(pairs)]
    for move in moves:
        move.start()
    gg_to[...] = gg[...].reshape(D)
    for move in moves:
        move.wait()


def layer(x, gain, w_key, w_value, w_query, w_out, gain_conv, taps, w_point, cot):
    bf, f32 = jnp.bfloat16, jnp.float32
    vmem = pl.BlockSpec(memory_space=pltpu.VMEM)
    hbm = pl.BlockSpec(memory_space=pl.ANY)
    dma = pltpu.SemaphoreType.DMA
    shapes = [((BLOCK, D), bf), ((BLOCK, D), bf), ((24, D), f32), ((KER, D), f32)]
    outs = [jax.ShapeDtypeStruct(*shape) for shape in shapes]
    scratch = [
        ((D, WIDE), bf), ((D, WIDE), bf), ((D, WIDE), bf), ((WIDE, D), bf), ((D, D), bf),
        ((BLOCK, D), bf),
        ((HEADS, 192, 128), bf), ((HEADS, 96, 128), bf),
        ((16, 208, HALF), bf), ((96, 1024), bf), ((112, 1024), f32), ((8, 1024), f32),
        ((96, 1024), bf), ((WIDE, 128), bf), ((8 * BLOCK, D), bf),
        ((BLOCK, D), bf), ((12, BLOCK, 128), f32), ((12, 160, 128), f32), ((12, BLOCK, 128), f32),
        ((12, 160, 128), f32), ((12, BLOCK, 128), f32), ((BLOCK, D), bf), ((D, BLOCK), f32),
        ((8, 192, 128), bf), ((192, 1024), bf), ((4, 16, D), bf), ((4, 16, D), bf),
        ((2, 4, 48, 768), bf), ((2, 3, 48, 768), bf), ((2, 2, 48, 384), bf), ((2, 4, 48, 384), bf),
        ((2, BLOCK, 128), f32), ((512, 128), f32), ((512, 128), bf), ((7, 64, 128), bf),
        ((4, 64, 128), bf), ((4, 64, 128), bf), ((512, 128), bf),
    ]
    counts = [10, 8, 8, 8, 8, 8, 8, 14, 14, 7, 7, 4, 4, 7, 7, 7, 7, 3, 3, 3, 3, 7, 7, 6, 6, 6, 6]
    results = pl.pallas_call(
        layer_kernel,
        name="layer",
        out_shape=tuple(outs + [jax.ShapeDtypeStruct((1, D), f32)]),
        in_specs=[vmem, vmem, hbm, hbm, hbm, hbm, vmem, vmem, hbm, vmem],
        out_specs=(vmem,) * 5,
        scratch_shapes=[pltpu.VMEM(*shape) for shape in scratch] + [dma((n,)) for n in counts],
        compiler_params=pltpu.CompilerParams(
            collective_id=0, has_side_effects=True, vmem_limit_bytes=60 << 20
        ),
        cost_estimate=pl.CostEstimate(
            flops=9 * 10**9, bytes_accessed=16 * 2**20, transcendentals=2**23
        ),
    )(x, gain, w_key, w_value, w_query, w_out, gain_conv, taps, w_point, cot)
    return pl.pallas_call(
        finish_kernel,
        name="finish",
        out_shape=tuple(outs + [jax.ShapeDtypeStruct((D,), f32)]),
        in_specs=[vmem] * 5,
        out_specs=(hbm,) * 4 + (vmem,),
        scratch_shapes=[dma((4,))],
    )(*results)


def on_device(
    inputs,
    attention_norm_gain,
    w_query,
    w_key,
    w_value,
    w_out,
    gain_conv,
    kernel,
    w_point,
    cotangent,
):
    layer_out, grad_hidden, grad_point, grad_kernel, grad_gain = layer(
        inputs[0], attention_norm_gain, w_key, w_value, w_query, w_out,
        gain_conv, kernel, w_point, cotangent[0],
    )
    return layer_out[None], grad_hidden[None], grad_point, grad_kernel, grad_gain


def solution(mesh):
    placed = (P("utt", "seq", None), P(), P(), P(), P(), P(), P(), P(), P(), P("utt", "seq", None))
    return jax.shard_map(
        on_device,
        mesh=mesh,
        in_specs=placed,
        out_specs=(P("utt", "seq", None), P("utt", "seq", None), P("seq", None), P(), P()),
        check_vma=False,
    )
```

```python
import math

import jax
import jax.numpy as jnp
from jax import lax
from jax.experimental import pallas as pl
from jax.experimental.pallas import tpu as pltpu
from jax.sharding import PartitionSpec as P

D = 1536
HEADS = 8
HEAD_DIM = 96
WIDE = HEADS * HEAD_DIM
KER = 32
BLOCK = 128
HALF = 512
LOG2E = 1.4426950408889634

OWN, SIB, ZM, ZP, Z2, SIB_ZM, SIB_ZP, SIB_Z2 = range(8)


def rows_norm(values):
    mean = jnp.mean(values, axis=-1, keepdims=True)
    centered = values - mean
    rstd = lax.rsqrt(jnp.mean(centered * centered, axis=-1, keepdims=True) + 1e-05)
    return centered * rstd, rstd


def matmul(a, b, da=1, db=0):
    return lax.dot_general(a, b, (((da,), (db,)), ((), ())), preferred_element_type=jnp.float32)


def layer_kernel(
    x_ref, gain_ref, wk_hbm, wv_hbm, wq_hbm, wo_hbm, gain_conv_ref, taps_ref, wp_hbm, cot_ref,
    out_ref, gh_ref, gp_ref, gk_ref, gg_ref,
    wk, wv, wq, wo, wp, normed, kv_out, q_out, kv, qt, acc, top, mix_out, mixt, cots,
    hidden, hhat, ci, back, dz, conv, act, act_t, act_out, act_in, edge, halo, tile_out, tile_in,
    y_out, y_in, part, gain_sum, b_out, b_in, c_in, d_in, total, n_group, n_z, n_y,
    gh_rows, out_rows,
    w_sem, kv_send, kv_recv, q_send, q_recv, m_send, m_recv, r_send, r_recv, s_send, s_recv,
    e_send, e_recv, a_send, a_recv, b_send, b_recv, c_send, c_recv, d_send, d_recv,
    g_send, g_recv, t_send, t_recv, y_send, y_recv, n_send, n_recv, o_sem,
):
    f32, bf = jnp.float32, jnp.bfloat16
    s = lax.axis_index("seq")
    u = lax.axis_index("utt")
    z, y_hi, x, c = s // 16, (s // 8) % 2, (s // 2) % 4, s % 2
    h, p, y = y_hi * 4 + x, s % 8, y_hi * 2 + u

    def dev(zz, hh, cc):
        return {"seq": zz * 16 + hh * 2 + cc}

    def plane(side, step, sign=1):
        return (y_hi + side) % 2 * 4 + (x + sign * step + 4) % 4

    near = [(0, 1), (0, 2), (0, 3)]
    away = [(1, 0), (1, 1), (1, 2), (1, 3)]
    up, down, sibling = dev((z + 1) % 4, h, c), dev((z + 3) % 4, h, c), dev(z, h, 1 - c)
    right, left = {"seq": (s + 1) % 64}, {"seq": (s + 63) % 64}
    group = [{"seq": s // 8 * 8 + (p + k) % 8} for k in range(1, 8)]
    z_peers = [dev((z + k) % 4, h, c) for k in range(1, 4)]
    y_peers = [
        {"seq": z * 16 + (y + k) % 4 // 2 * 8 + p, "utt": (y + k) % 4 % 2} for k in range(1, 4)
    ]
    copies = []

    def remote(src, dst, send, recv, to):
        copy = pltpu.make_async_remote_copy(
            src_ref=src, dst_ref=dst, send_sem=send, recv_sem=recv,
            device_id=to, device_id_type=pl.DeviceIdType.MESH,
        )
        copy.start()
        copies.append(copy)
        return copy

    def arrive(group_of_copies):
        for copy in group_of_copies:
            copy.wait_recv()

    loads = {}
    sem = 0
    for name, src, dst, cuts in (
        ("k", wk_hbm, wk, 2), ("v", wv_hbm, wv, 2), ("q", wq_hbm, wq, 2),
        ("p", wp_hbm, wp, 2), ("o", wo_hbm, wo, 2),
    ):
        rows = dst.shape[0] // cuts
        loads[name] = []
        for i in range(cuts):
            cut = pl.ds(i * rows, rows)
            loads[name].append(pltpu.make_async_copy(src.at[cut], dst.at[cut], w_sem.at[sem]))
            if name in "kvq":
                loads[name][-1].start()
            sem += 1

    def loaded(name):
        for load in loads[name]:
            load.wait()

    for slot in range(16):
        kv[slot, 192:208, :] = jnp.ones((16, HALF), bf)
    barrier = pltpu.get_barrier_semaphore()
    greeted = [dev(z, plane(a, b), c) for a, b in near + away] + group + z_peers + y_peers
    greeted += [right, left]
    for to in greeted:
        pl.semaphore_signal(barrier, inc=1, device_id=to, device_id_type=pl.DeviceIdType.MESH)

    xhat, unused_item = rows_norm(x_ref[...].astype(f32))
    normed[...] = (xhat * gain_ref[...].reshape(1, D)).astype(bf)
    loaded("k")
    rows = matmul(normed[...], wk[...]).T.astype(bf)
    for i in range(HEADS):
        kv_out[i, 0:96, :] = rows[i * 96 : i * 96 + 96, :]
    loaded("v")
    rows = matmul(normed[...], wv[...]).T.astype(bf)
    for i in range(HEADS):
        kv_out[i, 96:192, :] = rows[i * 96 : i * 96 + 96, :]
    pl.semaphore_wait(barrier, len(greeted))
    mine = pl.ds(pl.multiple_of(x * 128, 128), 128)
    lanes = pl.ds(pl.multiple_of(h * 128, 128), 128)

    def exchange(src, dst, send, recv, peers):
        made = []
        for a, b in peers:
            to = plane(a, b)
            made.append(remote(src(to), dst, send.at[4 * a + b], recv.at[4 * a + b], dev(z, to, c)))
        return made

    kv_near = exchange(lambda i: kv_out.at[i], kv.at[y_hi, 0:192, mine], kv_send, kv_recv, near)
    kv_away = exchange(lambda i: kv_out.at[i], kv.at[y_hi, 0:192, mine], kv_send, kv_recv, away)
    kv[y_hi, 0:192, mine] = kv_out[h]
    loaded("q")
    for load in loads["p"] + loads["o"]:
        load.start()
    rows = (matmul(normed[...], wq[...]) * (LOG2E / math.sqrt(HEAD_DIM))).T.astype(bf)
    for i in range(HEADS):
        q_out[i] = rows[i * 96 : i * 96 + 96, :]
    q_near = exchange(lambda i: q_out.at[i], qt.at[:, lanes], q_send, q_recv, near)
    q_away = exchange(lambda i: q_out.at[i], qt.at[:, lanes], q_send, q_recv, away)
    qt[:, lanes] = q_out[h]
    acc[...] = jnp.zeros_like(acc)
    top[...] = jnp.full_like(top, -1e30)

    NEAR, AWAY = y_hi, 1 - y_hi
    hops = []

    def forward(slot, half, to, to_slot):
        i = len(hops)
        copy = remote(kv.at[2 * slot + half, 0:192], kv.at[2 * to_slot + half, 0:192],
                      r_send.at[i], r_recv.at[i], to)
        hops.append(copy)
        return copy

    def attend(side, *halves):
        span = pl.ds(pl.multiple_of(side * HALF, HALF), HALF)
        halves = [2 * slot + half for slot, half in halves]
        scores = [matmul(kv[i, 0:96, :], qt[:, span], 0, 0) for i in halves]
        before = top[0:1, span]
        newest = before
        for one in scores:
            newest = jnp.maximum(newest, jnp.max(one, axis=0, keepdims=True))
        result = acc[:, span] * jnp.exp2(before - newest)
        for i, one in zip(halves, scores):
            result += matmul(kv[i, 96:208, :], jnp.exp2(one - newest).astype(bf))
        acc[:, span] = result
        top[0:1, span] = newest

    def attend_both(*halves):
        def one_side(side, carry):
            attend(side, *halves)
            return carry

        lax.fori_loop(0, 2, one_side, 0)

    arrive(kv_near)
    zm_n = forward(OWN, NEAR, up, ZM)
    zp_n = forward(OWN, NEAR, down, ZP)
    sib_n = forward(OWN, NEAR, sibling, SIB)
    loaded("p")
    grads = matmul(cot_ref[...], wp[...], 1, 1)
    for l in range(12):
        back[l] = grads[:, l * 128 : l * 128 + 128]
    arrive(kv_away)
    zp_a = forward(OWN, AWAY, down, ZP)
    zm_a = forward(OWN, AWAY, up, ZM)
    sib_a = forward(OWN, AWAY, sibling, SIB)
    arrive(q_near)
    sib_n.wait_recv()
    attend(NEAR, (OWN, NEAR), (SIB, NEAR))
    arrive(q_away)
    own_rows = pl.ds(pl.multiple_of(p * BLOCK, BLOCK), BLOCK)
    cots[own_rows, :] = cot_ref[...]
    ahead, behind = dev(z, plane(0, 1), c), dev(z, plane(0, 3), c)

    def cot_rows(step, first=0, count=BLOCK):
        start = ((x + step) % 4 * 2 + c) * BLOCK + first
        return cots.at[pl.ds(pl.multiple_of(start, 64), count)]

    def cot_send(i, src, to):
        return remote(src, src, s_send.at[i], s_recv.at[i], to)

    cot_ahead = cot_send(0, cot_rows(0), ahead)
    cot_behind = cot_send(1, cot_rows(0), behind)
    cot_relays = [cot_send(2, cot_rows(0), sibling)]
    attend(AWAY, (OWN, NEAR), (SIB, NEAR))
    sib_a.wait_recv()
    attend_both((OWN, AWAY), (SIB, AWAY))
    zm_n.wait_recv()
    z2_n = forward(ZM, NEAR, up, Z2)
    szm_n = forward(ZM, NEAR, sibling, SIB_ZM)
    zp_n.wait_recv()
    szp_n = forward(ZP, NEAR, sibling, SIB_ZP)
    attend_both((ZM, NEAR), (ZP, NEAR))
    zp_a.wait_recv()
    z2_a = forward(ZP, AWAY, down, Z2)
    szp_a = forward(ZP, AWAY, sibling, SIB_ZP)
    zm_a.wait_recv()
    szm_a = forward(ZM, AWAY, sibling, SIB_ZM)
    arrive([szm_n, szp_n])
    attend_both((SIB_ZM, NEAR), (SIB_ZP, NEAR), (ZM, AWAY), (ZP, AWAY))
    z2_n.wait_recv()
    sz2_n = forward(Z2, NEAR, sibling, SIB_Z2)
    z2_a.wait_recv()
    sz2_a = forward(Z2, AWAY, sibling, SIB_Z2)
    arrive([szm_a, szp_a])
    cot_ahead.wait_recv()
    cot_first = cot_send(3, cot_rows(3, 0, 64), ahead)
    cot_behind.wait_recv()
    cot_second = cot_send(4, cot_rows(1, 64, 64), behind)
    cot_relays += [cot_send(5, cot_rows(3), sibling), cot_send(6, cot_rows(1), sibling)]
    attend_both((SIB_ZM, AWAY), (SIB_ZP, AWAY), (Z2, NEAR), (Z2, AWAY))
    arrive([sz2_n, sz2_a])
    band = pl.ds(pl.multiple_of(h * 96, 96), 96)

    def give_back(side, peers):
        span = pl.ds(pl.multiple_of(side * HALF, HALF), HALF)
        mix_out[:, span] = (acc[0:96, span] / acc[96:97, span]).astype(bf)
        return exchange(
            lambda i: mix_out.at[:, pl.ds(pl.multiple_of(i * 128, 128), 128)],
            mixt.at[band, :], m_send, m_recv, peers,
        )

    attend(AWAY, (SIB_Z2, NEAR), (SIB_Z2, AWAY))
    m_away = give_back(AWAY, away)
    attend(NEAR, (SIB_Z2, NEAR), (SIB_Z2, AWAY))
    m_near = give_back(NEAR, near)
    mixt[band, :] = mix_out[:, lanes]
    loaded("o")
    arrive(m_away + m_near)
    hidden[...] = (x_ref[...].astype(f32) + matmul(mixt[...], wo[...], 0, 0)).astype(bf)

    standard, rstd = rows_norm(hidden[...].astype(f32))
    conv_in = (standard * gain_conv_ref[...].reshape(1, D)).astype(bf)
    edge[0] = conv_in[BLOCK - 16 :, :]
    edge[1] = conv_in[:16, :]
    halos = [
        remote(edge.at[0], halo.at[0], e_send.at[0], e_recv.at[0], right),
        remote(edge.at[1], halo.at[1], e_send.at[1], e_recv.at[1], left),
    ]
    for l in range(12):
        hhat[l] = standard[:, l * 128 : l * 128 + 128]
        ci[l, 16:144, :] = conv_in[:, l * 128 : l * 128 + 128].astype(f32)

    def place_halo(ref, slot):
        low = jnp.where(s > 0, halo[slot].astype(f32), 0.0)
        high = jnp.where(s < 63, halo[slot + 1].astype(f32), 0.0)
        for l in range(12):
            ref[l, 0:16, :] = low[:, l * 128 : l * 128 + 128]
            ref[l, 144:160, :] = high[:, l * 128 : l * 128 + 128]

    def span_of(l):
        return pl.ds(pl.multiple_of(l * 128, 128), 128)

    def conv_rows(l, first, count):
        result = jnp.zeros((count, 128), f32)
        for j in range(KER):
            result += taps_ref[j : j + 1, span_of(l)] * ci[l, first + j : first + j + count, :]
        conv[l, first : first + count, :] = result

    def grad_rows(l, first, count):
        result = jnp.zeros((count, 128), f32)
        for j in range(KER):
            start = first + 32 - j
            result += taps_ref[j : j + 1, span_of(l)] * dz[l, start : start + count, :]
        return result

    def middle(l, carry):
        conv_rows(l, 16, 96)
        return carry

    lax.fori_loop(0, 12, middle, 0)
    arrive([cot_first, cot_second])
    cot_relays.append(cot_send(7, cot_rows(2), sibling))
    arrive(halos)
    place_halo(ci, 0)

    def activate(l, carry):
        conv_rows(l, 0, 16)
        conv_rows(l, 112, 16)
        value = conv[l]
        sig = 1.0 / (1.0 + jnp.exp(-value))
        rounded = (value * sig).astype(bf)
        act[:, span_of(l)] = rounded
        act_t[span_of(l), :] = rounded.astype(f32).T
        dz[l, 16:144, :] = back[l] * (sig * (1.0 + value * (1.0 - sig)))
        return carry

    own_lanes = pl.ds(pl.multiple_of(p * 128, 128), 128)
    act_copies = []

    def send_act(i):
        for to in range(8):
            starts = [24 * (8 * b + to) for b in range(4 * i, 4 * i + 4)]
            pieces = [act_t[start : start + 24, :] for start in starts]
            act_out[i, to] = jnp.concatenate(pieces, axis=0).astype(bf)
        act_copies.append([
            remote(act_out.at[i, (p + k) % 8], act_in.at[i, :, own_lanes],
                   a_send.at[7 * i + k - 1], a_recv.at[7 * i + k - 1], group[k - 1])
            for k in range(1, 8)
        ])
        act_in[i, :, own_lanes] = act_out[i, p]

    lax.fori_loop(0, 6, activate, 0)
    send_act(0)
    lax.fori_loop(6, 12, activate, 0)
    for l in range(12):
        edge[2, :, l * 128 : l * 128 + 128] = dz[l, 128:144, :].astype(bf)
        edge[3, :, l * 128 : l * 128 + 128] = dz[l, 16:32, :].astype(bf)
    halos = [
        remote(edge.at[2], halo.at[2], e_send.at[2], e_recv.at[2], right),
        remote(edge.at[3], halo.at[3], e_send.at[3], e_recv.at[3], left),
    ]
    send_act(1)

    def taps_grad(l, carry):
        grad = dz[l, 16:144, :]
        for j0 in range(0, KER, 16):
            rows = [
                jnp.sum(grad * ci[l, j : j + BLOCK, :], axis=0, keepdims=True)
                for j in range(j0, j0 + 16)
            ]
            at = pl.ds(pl.multiple_of(l * KER + j0, 16), 16)
            b_out[at, :] = jnp.concatenate(rows, axis=0).astype(bf)
        return carry

    lax.fori_loop(0, 12, taps_grad, 0)
    share = 12 * KER // 8

    def share_of(i):
        return pl.ds(pl.multiple_of(i * share, share), share)

    b_copies = [
        remote(b_out.at[share_of((p + k) % 8)], b_in.at[k - 1],
               b_send.at[k - 1], b_recv.at[k - 1], group[k - 1])
        for k in range(1, 8)
    ]

    t_copies = []

    def tile_rows(i):
        arrive(act_copies[i])
        for j in range(2):
            tile = matmul(act_in[i], cots[:, j * 768 : j * 768 + 768])
            for b in range(2):
                tile_out[j, 2 * i + b] = tile[48 * b : 48 * b + 48, :].astype(bf)
            for b in range(2):
                to = 2 * i + b
                sent = pltpu.make_async_remote_copy(
                    src_ref=tile_out.at[j, to], dst_ref=tile_in.at[j, z],
                    send_sem=t_send.at[4 * j + to], recv_sem=t_recv.at[4 * j + z],
                    device_id=dev(to, h, c), device_id_type=pl.DeviceIdType.MESH,
                )
                t_copies.append((to, sent))

                @pl.when(z != to)
                def _():
                    sent.start()

    arrive(cot_relays)
    tile_rows(0)
    arrive(b_copies)
    c_in[z] = sum([b_out[share_of(p), :].astype(f32)] + [b_in[k].astype(f32) for k in range(7)]).astype(bf)
    c_copies = [
        remote(c_in.at[z], c_in.at[z], c_send.at[k], c_recv.at[k], z_peers[k]) for k in range(3)
    ]
    tile_rows(1)

    arrive(halos)
    place_halo(dz, 2)
    part[...] = jnp.zeros_like(part)
    gain_sum[...] = jnp.zeros_like(gain_sum)

    def backward(l, carry):
        grad = grad_rows(l, 0, BLOCK)
        gain_sum[pl.ds(l, 1), :] = jnp.sum(grad * hhat[l], axis=0, keepdims=True)
        g = grad * gain_conv_ref[span_of(l)].reshape(1, 128)
        back[l] = g
        part[0] += g
        part[1] += g * hhat[l]
        return carry

    lax.fori_loop(0, 12, backward, 0)

    def spread(ref, at, base, peers, value):
        ref[at] = value
        return [
            remote(ref.at[at], ref.at[at], n_send.at[base + k], n_recv.at[base + k], to)
            for k, to in enumerate(peers)
        ]

    n_copies = spread(n_group, p, 0, group, gain_sum[...])
    arrive(c_copies)
    d_in[y] = sum(c_in[k].astype(f32) for k in range(4)).astype(bf)
    d_copies = [
        remote(d_in.at[y], d_in.at[y], d_send.at[k], d_recv.at[k], y_peers[k]) for k in range(3)
    ]
    mean_g = jnp.sum(part[0], axis=-1, keepdims=True) * (1.0 / D)
    mean_gh = jnp.sum(part[1], axis=-1, keepdims=True) * (1.0 / D)
    for l in range(12):
        cut = slice(l * 128, l * 128 + 128)
        inner = back[l] - mean_g - hhat[l] * mean_gh
        gh_rows[:, cut] = (cot_ref[:, cut].astype(f32) + rstd * inner).astype(bf)
    gh_store = pltpu.make_async_copy(gh_rows, gh_ref, o_sem.at[0])
    gh_store.start()
    arrive(n_copies)
    n_copies = spread(n_z, z, 7, z_peers, sum(n_group[k] for k in range(8)))
    arrive(d_copies)
    total[share_of(p), :] = sum(d_in[k].astype(f32) for k in range(4)).astype(bf)
    g_copies = [
        remote(total.at[share_of(p)], total.at[share_of(p)], g_send.at[k], g_recv.at[k], group[k])
        for k in range(7)
    ]
    out_rows[...] = (hidden[...].astype(f32) + matmul(act[...], wp[...])).astype(bf)
    out_store = pltpu.make_async_copy(out_rows, out_ref, o_sem.at[1])
    out_store.start()
    arrive(n_copies)
    n_copies = spread(n_y, y, 10, y_peers, sum(n_z[k] for k in range(4)))
    y_copies = []

    def along_y(i):
        for k in range(4):
            got = pltpu.make_async_remote_copy(
                src_ref=tile_out.at[i, k], dst_ref=tile_in.at[i, k],
                send_sem=t_send.at[4 * i + k], recv_sem=t_recv.at[4 * i + k],
                device_id=dev(k, h, c), device_id_type=pl.DeviceIdType.MESH,
            )

            @pl.when(z != k)
            def _():
                got.wait_recv()

        tile_in[i, z] = tile_out[i, z]
        mixed = sum(tile_in[i, k].astype(f32) for k in range(4))
        for b in range(2):
            rows = mixed[24 * b : 24 * b + 24, :]
            y_out[i, b] = jnp.concatenate([rows[:, :384], rows[:, 384:]], axis=0).astype(bf)
        y_copies.append([
            remote(y_out.at[i, (y + k) % 4 // 2], y_in.at[i, y],
                   y_send.at[3 * i + k - 1], y_recv.at[3 * i + k - 1], y_peers[k - 1])
            for k in range(1, 4)
        ])
        y_in[i, y] = y_out[i, y_hi]

    along_y(0)
    along_y(1)
    scale = 1.0 / math.sqrt(2 * 64 * BLOCK)
    arrive(g_copies)
    arrive(n_copies)
    gain_total = sum(n_y[k] for k in range(4)) * scale
    for l in range(12):
        cut = slice(l * 128, l * 128 + 128)
        gk_ref[:, cut] = total[l * KER : l * KER + KER, :].astype(f32) * scale
        gg_ref[:, cut] = gain_total[l : l + 1, :]
    for i in range(2):
        arrive(y_copies[i])
        whole = sum(y_in[i, k].astype(f32) for k in range(4)) * scale
        gp_ref[:, i * 768 : i * 768 + 384] = whole[:24, :]
        gp_ref[:, i * 768 + 384 : i * 768 + 768] = whole[24:, :]
    gh_store.wait()
    out_store.wait()
    for to, sent in t_copies:

        @pl.when(z != to)
        def _():
            sent.wait_send()

    for copy in copies:
        copy.wait_send()


def finish_kernel(out, gh, gp, gk, gg, out_to, gh_to, gp_to, gk_to, gg_to, sem):
    pairs = ((out, out_to), (gh, gh_to), (gp, gp_to), (gk, gk_to))
    moves = [pltpu.make_async_copy(src, dst, sem.at[i]) for i, (src, dst) in enumerate(pairs)]
    for move in moves:
        move.start()
    gg_to[...] = gg[...].reshape(D)
    for move in moves:
        move.wait()


def layer(x, gain, w_key, w_value, w_query, w_out, gain_conv, taps, w_point, cot):
    bf, f32 = jnp.bfloat16, jnp.float32
    vmem = pl.BlockSpec(memory_space=pltpu.VMEM)
    hbm = pl.BlockSpec(memory_space=pl.ANY)
    dma = pltpu.SemaphoreType.DMA
    shapes = [((BLOCK, D), bf), ((BLOCK, D), bf), ((24, D), f32), ((KER, D), f32)]
    outs = [jax.ShapeDtypeStruct(*shape) for shape in shapes]
    scratch = [
        ((D, WIDE), bf), ((D, WIDE), bf), ((D, WIDE), bf), ((WIDE, D), bf), ((D, D), bf),
        ((BLOCK, D), bf),
        ((HEADS, 192, 128), bf), ((HEADS, 96, 128), bf),
        ((16, 208, HALF), bf), ((96, 1024), bf), ((112, 1024), f32), ((8, 1024), f32),
        ((96, 1024), bf), ((WIDE, 128), bf), ((8 * BLOCK, D), bf),
        ((BLOCK, D), bf), ((12, BLOCK, 128), f32), ((12, 160, 128), f32), ((12, BLOCK, 128), f32),
        ((12, 160, 128), f32), ((12, BLOCK, 128), f32), ((BLOCK, D), bf), ((D, BLOCK), f32),
        ((2, 8, 96, 128), bf), ((2, 96, 1024), bf), ((4, 16, D), bf), ((4, 16, D), bf),
        ((2, 4, 48, 768), bf), ((2, 4, 48, 768), bf), ((2, 2, 48, 384), bf), ((2, 4, 48, 384), bf),
        ((2, BLOCK, 128), f32), ((16, 128), f32), ((384, 128), bf), ((7, 48, 128), bf),
        ((4, 48, 128), bf), ((4, 48, 128), bf), ((384, 128), bf),
        ((8, 16, 128), f32), ((4, 16, 128), f32), ((4, 16, 128), f32),
        ((BLOCK, D), bf), ((BLOCK, D), bf),
    ]
    counts = [10, 8, 8, 8, 8, 8, 8, 14, 14, 8, 8, 4, 4, 14, 14, 7, 7, 3, 3, 3, 3, 7, 7, 8, 8, 6, 6]
    counts += [13, 13, 2]
    results = pl.pallas_call(
        layer_kernel,
        name="layer",
        out_shape=tuple(outs + [jax.ShapeDtypeStruct((1, D), f32)]),
        in_specs=[vmem, vmem, hbm, hbm, hbm, hbm, vmem, vmem, hbm, vmem],
        out_specs=(hbm, hbm, vmem, vmem, vmem),
        scratch_shapes=[pltpu.VMEM(*shape) for shape in scratch] + [dma((n,)) for n in counts],
        compiler_params=pltpu.CompilerParams(
            collective_id=0, has_side_effects=True, vmem_limit_bytes=60 << 20
        ),
        cost_estimate=pl.CostEstimate(
            flops=9 * 10**9, bytes_accessed=16 * 2**20, transcendentals=2**23
        ),
    )(x, gain, w_key, w_value, w_query, w_out, gain_conv, taps, w_point, cot)
    return pl.pallas_call(
        finish_kernel,
        name="finish",
        out_shape=tuple(outs + [jax.ShapeDtypeStruct((D,), f32)]),
        in_specs=[vmem] * 5,
        out_specs=(hbm,) * 4 + (vmem,),
        scratch_shapes=[dma((4,))],
    )(*results)


def on_device(
    inputs,
    attention_norm_gain,
    w_query,
    w_key,
    w_value,
    w_out,
    gain_conv,
    kernel,
    w_point,
    cotangent,
):
    layer_out, grad_hidden, grad_point, grad_kernel, grad_gain = layer(
        inputs[0], attention_norm_gain, w_key, w_value, w_query, w_out,
        gain_conv, kernel, w_point, cotangent[0],
    )
    return layer_out[None], grad_hidden[None], grad_point, grad_kernel, grad_gain


def solution(mesh):
    placed = (P("utt", "seq", None), P(), P(), P(), P(), P(), P(), P(), P(), P("utt", "seq", None))
    return jax.shard_map(
        on_device,
        mesh=mesh,
        in_specs=placed,
        out_specs=(P("utt", "seq", None), P("utt", "seq", None), P("seq", None), P(), P()),
        check_vma=False,
    )
```

```python
import math

import jax
import jax.numpy as jnp
from jax import lax
from jax.experimental import pallas as pl
from jax.experimental.pallas import tpu as pltpu
from jax.sharding import PartitionSpec as P

D = 1536
HEADS = 8
HEAD_DIM = 96
WIDE = HEADS * HEAD_DIM
KER = 32
BLOCK = 128
HALF = 512
LOG2E = 1.4426950408889634

OWN, SIB, ZM, ZP, Z2, SIB_ZM, SIB_ZP, SIB_Z2 = range(8)


def rows_norm(values):
    mean = jnp.mean(values, axis=-1, keepdims=True)
    centered = values - mean
    rstd = lax.rsqrt(jnp.mean(centered * centered, axis=-1, keepdims=True) + 1e-05)
    return centered * rstd, rstd


def matmul(a, b, da=1, db=0):
    return lax.dot_general(a, b, (((da,), (db,)), ((), ())), preferred_element_type=jnp.float32)


def layer_kernel(
    x_ref, gain_ref, wk_hbm, wv_hbm, wq_hbm, wo_hbm, gain_conv_ref, taps_ref, wp_hbm, cot_ref,
    out_ref, gh_ref, gp_ref, gk_ref, gg_ref,
    wk, wv, wq, wo, wp, normed, kv_out, q_out, kv, qt, acc, top, mix_out, mixt, cots,
    hidden, hhat, ci, back, dz, conv, act, act_t, act_out, act_in, edge, halo, tile_out, tile_in,
    y_out, y_in, part, gain_sum, b_out, b_in, c_in, d_in, total, n_group, n_z, n_y,
    gh_rows, out_rows,
    w_sem, kv_send, kv_recv, q_send, q_recv, m_send, m_recv, r_send, r_recv, s_send, s_recv,
    e_send, e_recv, a_send, a_recv, b_send, b_recv, c_send, c_recv, d_send, d_recv,
    g_send, g_recv, t_send, t_recv, y_send, y_recv, n_send, n_recv, o_sem,
):
    f32, bf = jnp.float32, jnp.bfloat16
    s = lax.axis_index("seq")
    u = lax.axis_index("utt")
    z, y_hi, x, c = s // 16, (s // 8) % 2, (s // 2) % 4, s % 2
    h, p, y = y_hi * 4 + x, s % 8, y_hi * 2 + u

    def dev(zz, hh, cc):
        return {"seq": zz * 16 + hh * 2 + cc}

    def plane(side, step, sign=1):
        return (y_hi + side) % 2 * 4 + (x + sign * step + 4) % 4

    near = [(0, 1), (0, 2), (0, 3)]
    away = [(1, 0), (1, 1), (1, 2), (1, 3)]
    up, down, sibling = dev((z + 1) % 4, h, c), dev((z + 3) % 4, h, c), dev(z, h, 1 - c)
    right, left = {"seq": (s + 1) % 64}, {"seq": (s + 63) % 64}
    group = [{"seq": s // 8 * 8 + (p + k) % 8} for k in range(1, 8)]
    z_peers = [dev((z + k) % 4, h, c) for k in range(1, 4)]
    y_peers = [
        {"seq": z * 16 + (y + k) % 4 // 2 * 8 + p, "utt": (y + k) % 4 % 2} for k in range(1, 4)
    ]
    copies = []

    def remote(src, dst, send, recv, to):
        copy = pltpu.make_async_remote_copy(
            src_ref=src, dst_ref=dst, send_sem=send, recv_sem=recv,
            device_id=to, device_id_type=pl.DeviceIdType.MESH,
        )
        copy.start()
        copies.append(copy)
        return copy

    def arrive(group_of_copies):
        for copy in group_of_copies:
            copy.wait_recv()

    loads = {}
    sem = 0
    for name, src, dst, cuts in (
        ("k", wk_hbm, wk, 2), ("v", wv_hbm, wv, 2), ("q", wq_hbm, wq, 2),
        ("p", wp_hbm, wp, 2), ("o", wo_hbm, wo, 2),
    ):
        rows = dst.shape[0] // cuts
        loads[name] = []
        for i in range(cuts):
            cut = pl.ds(i * rows, rows)
            loads[name].append(pltpu.make_async_copy(src.at[cut], dst.at[cut], w_sem.at[sem]))
            if name in "kvq":
                loads[name][-1].start()
            sem += 1

    def loaded(name):
        for load in loads[name]:
            load.wait()

    for slot in range(16):
        kv[slot, 192:208, :] = jnp.ones((16, HALF), bf)
    barrier = pltpu.get_barrier_semaphore()
    greeted = [dev(z, plane(a, b), c) for a, b in near + away] + group + z_peers + y_peers
    greeted += [right, left]
    for to in greeted:
        pl.semaphore_signal(barrier, inc=1, device_id=to, device_id_type=pl.DeviceIdType.MESH)

    xhat, unused_item = rows_norm(x_ref[...].astype(f32))
    normed[...] = (xhat * gain_ref[...].reshape(1, D)).astype(bf)
    loaded("k")
    rows = matmul(normed[...], wk[...]).T.astype(bf)
    for i in range(HEADS):
        kv_out[i, 0:96, :] = rows[i * 96 : i * 96 + 96, :]
    loaded("v")
    rows = matmul(normed[...], wv[...]).T.astype(bf)
    for i in range(HEADS):
        kv_out[i, 96:192, :] = rows[i * 96 : i * 96 + 96, :]
    pl.semaphore_wait(barrier, len(greeted))
    mine = pl.ds(pl.multiple_of(x * 128, 128), 128)
    lanes = pl.ds(pl.multiple_of(h * 128, 128), 128)

    def exchange(src, dst, send, recv, peers):
        made = []
        for a, b in peers:
            to = plane(a, b)
            made.append(remote(src(to), dst, send.at[4 * a + b], recv.at[4 * a + b], dev(z, to, c)))
        return made

    kv_near = exchange(lambda i: kv_out.at[i], kv.at[y_hi, 0:192, mine], kv_send, kv_recv, near)
    kv_away = exchange(lambda i: kv_out.at[i], kv.at[y_hi, 0:192, mine], kv_send, kv_recv, away)
    kv[y_hi, 0:192, mine] = kv_out[h]
    loaded("q")
    for load in loads["p"] + loads["o"]:
        load.start()
    rows = (matmul(normed[...], wq[...]) * (LOG2E / math.sqrt(HEAD_DIM))).T.astype(bf)
    for i in range(HEADS):
        q_out[i] = rows[i * 96 : i * 96 + 96, :]
    q_near = exchange(lambda i: q_out.at[i], qt.at[:, lanes], q_send, q_recv, near)
    q_away = exchange(lambda i: q_out.at[i], qt.at[:, lanes], q_send, q_recv, away)
    qt[:, lanes] = q_out[h]
    acc[...] = jnp.zeros_like(acc)
    top[...] = jnp.full_like(top, -1e30)

    NEAR, AWAY = y_hi, 1 - y_hi
    hops = []

    def forward(slot, half, to, to_slot):
        i = len(hops)
        copy = remote(kv.at[2 * slot + half, 0:192], kv.at[2 * to_slot + half, 0:192],
                      r_send.at[i], r_recv.at[i], to)
        hops.append(copy)
        return copy

    def attend(side, *halves):
        span = pl.ds(pl.multiple_of(side * HALF, HALF), HALF)
        halves = [2 * slot + half for slot, half in halves]
        scores = [matmul(kv[i, 0:96, :], qt[:, span], 0, 0) for i in halves]
        before = top[0:1, span]
        newest = before
        for one in scores:
            newest = jnp.maximum(newest, jnp.max(one, axis=0, keepdims=True))
        result = acc[:, span] * jnp.exp2(before - newest)
        for i, one in zip(halves, scores):
            result += matmul(kv[i, 96:208, :], jnp.exp2(one - newest).astype(bf))
        acc[:, span] = result
        top[0:1, span] = newest

    def attend_both(*halves):
        def one_side(side, carry):
            attend(side, *halves)
            return carry

        lax.fori_loop(0, 2, one_side, 0)

    arrive(kv_near)
    zm_n = forward(OWN, NEAR, up, ZM)
    zp_n = forward(OWN, NEAR, down, ZP)
    sib_n = forward(OWN, NEAR, sibling, SIB)
    loaded("p")
    grads = matmul(cot_ref[...], wp[...], 1, 1)
    for l in range(12):
        back[l] = grads[:, l * 128 : l * 128 + 128]
    arrive(kv_away)
    zp_a = forward(OWN, AWAY, down, ZP)
    zm_a = forward(OWN, AWAY, up, ZM)
    sib_a = forward(OWN, AWAY, sibling, SIB)
    arrive(q_near)
    sib_n.wait_recv()
    attend(NEAR, (OWN, NEAR), (SIB, NEAR))
    arrive(q_away)
    own_rows = pl.ds(pl.multiple_of(p * BLOCK, BLOCK), BLOCK)
    cots[own_rows, :] = cot_ref[...]
    ahead, behind = dev(z, plane(0, 1), c), dev(z, plane(0, 3), c)

    def cot_rows(step, first=0, count=BLOCK):
        start = ((x + step) % 4 * 2 + c) * BLOCK + first
        return cots.at[pl.ds(pl.multiple_of(start, 64), count)]

    def cot_send(i, src, to):
        return remote(src, src, s_send.at[i], s_recv.at[i], to)

    cot_ahead = cot_send(0, cot_rows(0), ahead)
    cot_behind = cot_send(1, cot_rows(0), behind)
    cot_relays = [cot_send(2, cot_rows(0), sibling)]
    attend(AWAY, (OWN, NEAR), (SIB, NEAR))
    sib_a.wait_recv()
    attend_both((OWN, AWAY), (SIB, AWAY))
    zm_n.wait_recv()
    z2_n = forward(ZM, NEAR, up, Z2)
    szm_n = forward(ZM, NEAR, sibling, SIB_ZM)
    zp_n.wait_recv()
    szp_n = forward(ZP, NEAR, sibling, SIB_ZP)
    attend_both((ZM, NEAR), (ZP, NEAR))
    zp_a.wait_recv()
    z2_a = forward(ZP, AWAY, down, Z2)
    szp_a = forward(ZP, AWAY, sibling, SIB_ZP)
    zm_a.wait_recv()
    szm_a = forward(ZM, AWAY, sibling, SIB_ZM)
    arrive([szm_n, szp_n])
    attend_both((SIB_ZM, NEAR), (SIB_ZP, NEAR), (ZM, AWAY), (ZP, AWAY))
    z2_n.wait_recv()
    sz2_n = forward(Z2, NEAR, sibling, SIB_Z2)
    z2_a.wait_recv()
    sz2_a = forward(Z2, AWAY, sibling, SIB_Z2)
    arrive([szm_a, szp_a])
    cot_ahead.wait_recv()
    cot_first = cot_send(3, cot_rows(3, 0, 64), ahead)
    cot_behind.wait_recv()
    cot_second = cot_send(4, cot_rows(1, 64, 64), behind)
    cot_relays += [cot_send(5, cot_rows(3), sibling), cot_send(6, cot_rows(1), sibling)]
    attend_both((SIB_ZM, AWAY), (SIB_ZP, AWAY), (Z2, NEAR), (Z2, AWAY))
    arrive([sz2_n, sz2_a])
    band = pl.ds(pl.multiple_of(h * 96, 96), 96)

    def give_back(side, peers):
        span = pl.ds(pl.multiple_of(side * HALF, HALF), HALF)
        mix_out[:, span] = (acc[0:96, span] / acc[96:97, span]).astype(bf)
        return exchange(
            lambda i: mix_out.at[:, pl.ds(pl.multiple_of(i * 128, 128), 128)],
            mixt.at[band, :], m_send, m_recv, peers,
        )

    attend(AWAY, (SIB_Z2, NEAR), (SIB_Z2, AWAY))
    m_away = give_back(AWAY, away)
    attend(NEAR, (SIB_Z2, NEAR), (SIB_Z2, AWAY))
    m_near = give_back(NEAR, near)
    mixt[band, :] = mix_out[:, lanes]
    loaded("o")
    arrive(m_away + m_near)
    hidden[...] = (x_ref[...].astype(f32) + matmul(mixt[...], wo[...], 0, 0)).astype(bf)

    standard, rstd = rows_norm(hidden[...].astype(f32))
    conv_in = (standard * gain_conv_ref[...].reshape(1, D)).astype(bf)
    edge[0] = conv_in[BLOCK - 16 :, :]
    edge[1] = conv_in[:16, :]
    halos = [
        remote(edge.at[0], halo.at[0], e_send.at[0], e_recv.at[0], right),
        remote(edge.at[1], halo.at[1], e_send.at[1], e_recv.at[1], left),
    ]
    for l in range(12):
        hhat[l] = standard[:, l * 128 : l * 128 + 128]
        ci[l, 16:144, :] = conv_in[:, l * 128 : l * 128 + 128].astype(f32)

    def place_halo(ref, slot):
        low = jnp.where(s > 0, halo[slot].astype(f32), 0.0)
        high = jnp.where(s < 63, halo[slot + 1].astype(f32), 0.0)
        for l in range(12):
            ref[l, 0:16, :] = low[:, l * 128 : l * 128 + 128]
            ref[l, 144:160, :] = high[:, l * 128 : l * 128 + 128]

    def span_of(l):
        return pl.ds(pl.multiple_of(l * 128, 128), 128)

    def conv_rows(l, first, count):
        result = jnp.zeros((count, 128), f32)
        for j in range(KER):
            result += taps_ref[j : j + 1, span_of(l)] * ci[l, first + j : first + j + count, :]
        conv[l, first : first + count, :] = result

    def grad_rows(l, first, count):
        result = jnp.zeros((count, 128), f32)
        for j in range(KER):
            start = first + 32 - j
            result += taps_ref[j : j + 1, span_of(l)] * dz[l, start : start + count, :]
        return result

    def middle(l, carry):
        conv_rows(l, 16, 96)
        return carry

    lax.fori_loop(0, 12, middle, 0)
    arrive([cot_first, cot_second])
    cot_relays.append(cot_send(7, cot_rows(2), sibling))
    arrive(halos)
    place_halo(ci, 0)

    def activate(l, carry):
        conv_rows(l, 0, 16)
        conv_rows(l, 112, 16)
        value = conv[l]
        sig = 1.0 / (1.0 + jnp.exp(-value))
        rounded = (value * sig).astype(bf)
        act[:, span_of(l)] = rounded
        act_t[span_of(l), :] = rounded.astype(f32).T
        dz[l, 16:144, :] = back[l] * (sig * (1.0 + value * (1.0 - sig)))
        return carry

    own_lanes = pl.ds(pl.multiple_of(p * 128, 128), 128)
    act_copies = []

    def send_act(i):
        for to in range(8):
            starts = [24 * (8 * b + to) for b in range(4 * i, 4 * i + 4)]
            pieces = [act_t[start : start + 24, :] for start in starts]
            act_out[i, to] = jnp.concatenate(pieces, axis=0).astype(bf)
        act_copies.append([
            remote(act_out.at[i, (p + k) % 8], act_in.at[i, :, own_lanes],
                   a_send.at[7 * i + k - 1], a_recv.at[7 * i + k - 1], group[k - 1])
            for k in range(1, 8)
        ])
        act_in[i, :, own_lanes] = act_out[i, p]

    lax.fori_loop(0, 6, activate, 0)
    send_act(0)
    lax.fori_loop(6, 12, activate, 0)
    for l in range(12):
        edge[2, :, l * 128 : l * 128 + 128] = dz[l, 128:144, :].astype(bf)
        edge[3, :, l * 128 : l * 128 + 128] = dz[l, 16:32, :].astype(bf)
    halos = [
        remote(edge.at[2], halo.at[2], e_send.at[2], e_recv.at[2], right),
        remote(edge.at[3], halo.at[3], e_send.at[3], e_recv.at[3], left),
    ]
    send_act(1)

    def taps_grad(l, carry):
        grad = dz[l, 16:144, :]
        for j0 in range(0, KER, 16):
            rows = [
                jnp.sum(grad * ci[l, j : j + BLOCK, :], axis=0, keepdims=True)
                for j in range(j0, j0 + 16)
            ]
            at = pl.ds(pl.multiple_of(l * KER + j0, 16), 16)
            b_out[at, :] = jnp.concatenate(rows, axis=0).astype(bf)
        return carry

    lax.fori_loop(0, 12, taps_grad, 0)
    share = 12 * KER // 8

    def share_of(i):
        return pl.ds(pl.multiple_of(i * share, share), share)

    b_copies = [
        remote(b_out.at[share_of((p + k) % 8)], b_in.at[k - 1],
               b_send.at[k - 1], b_recv.at[k - 1], group[k - 1])
        for k in range(1, 8)
    ]

    def spread(ref, at, base, peers, value):
        ref[at] = value
        return [
            remote(ref.at[at], ref.at[at], n_send.at[base + k], n_recv.at[base + k], to)
            for k, to in enumerate(peers)
        ]

    t_copies = []

    def tile_rows(i):
        arrive(act_copies[i])
        for j in range(2):
            tile = matmul(act_in[i], cots[:, j * 768 : j * 768 + 768])
            for b in range(2):
                tile_out[j, 2 * i + b] = tile[48 * b : 48 * b + 48, :].astype(bf)
            for b in range(2):
                to = 2 * i + b
                sent = pltpu.make_async_remote_copy(
                    src_ref=tile_out.at[j, to], dst_ref=tile_in.at[j, z],
                    send_sem=t_send.at[4 * j + to], recv_sem=t_recv.at[4 * j + z],
                    device_id=dev(to, h, c), device_id_type=pl.DeviceIdType.MESH,
                )
                t_copies.append((to, sent))

                @pl.when(z != to)
                def _():
                    sent.start()

    y_copies = []

    def along_y(i):
        for k in range(4):
            got = pltpu.make_async_remote_copy(
                src_ref=tile_out.at[i, k], dst_ref=tile_in.at[i, k],
                send_sem=t_send.at[4 * i + k], recv_sem=t_recv.at[4 * i + k],
                device_id=dev(k, h, c), device_id_type=pl.DeviceIdType.MESH,
            )

            @pl.when(z != k)
            def _():
                got.wait_recv()

        tile_in[i, z] = tile_out[i, z]
        mixed = sum(tile_in[i, k].astype(f32) for k in range(4))
        for b in range(2):
            rows = mixed[24 * b : 24 * b + 24, :]
            y_out[i, b] = jnp.concatenate([rows[:, :384], rows[:, 384:]], axis=0).astype(bf)
        y_copies.append([
            remote(y_out.at[i, (y + k) % 4 // 2], y_in.at[i, y],
                   y_send.at[3 * i + k - 1], y_recv.at[3 * i + k - 1], y_peers[k - 1])
            for k in range(1, 4)
        ])
        y_in[i, y] = y_out[i, y_hi]

    out_rows[...] = (hidden[...].astype(f32) + matmul(act[...], wp[...])).astype(bf)
    out_store = pltpu.make_async_copy(out_rows, out_ref, o_sem.at[1])
    out_store.start()
    arrive(cot_relays)
    tile_rows(0)
    arrive(b_copies)
    c_in[z] = sum([b_out[share_of(p), :].astype(f32)] + [b_in[k].astype(f32) for k in range(7)]).astype(bf)
    c_copies = [
        remote(c_in.at[z], c_in.at[z], c_send.at[k], c_recv.at[k], z_peers[k]) for k in range(3)
    ]
    tile_rows(1)
    arrive(halos)
    place_halo(dz, 2)
    part[...] = jnp.zeros_like(part)
    gain_sum[...] = jnp.zeros_like(gain_sum)

    def backward(l, carry):
        grad = grad_rows(l, 0, BLOCK)
        gain_sum[pl.ds(l, 1), :] = jnp.sum(grad * hhat[l], axis=0, keepdims=True)
        g = grad * gain_conv_ref[span_of(l)].reshape(1, 128)
        back[l] = g
        part[0] += g
        part[1] += g * hhat[l]
        return carry

    lax.fori_loop(0, 12, backward, 0)

    n_copies = spread(n_group, p, 0, group, gain_sum[...])
    arrive(c_copies)
    d_in[y] = sum(c_in[k].astype(f32) for k in range(4)).astype(bf)
    d_copies = [
        remote(d_in.at[y], d_in.at[y], d_send.at[k], d_recv.at[k], y_peers[k]) for k in range(3)
    ]
    mean_g = jnp.sum(part[0], axis=-1, keepdims=True) * (1.0 / D)
    mean_gh = jnp.sum(part[1], axis=-1, keepdims=True) * (1.0 / D)
    for l in range(12):
        cut = slice(l * 128, l * 128 + 128)
        inner = back[l] - mean_g - hhat[l] * mean_gh
        gh_rows[:, cut] = (cot_ref[:, cut].astype(f32) + rstd * inner).astype(bf)
    gh_store = pltpu.make_async_copy(gh_rows, gh_ref, o_sem.at[0])
    gh_store.start()
    arrive(n_copies)
    n_copies = spread(n_z, z, 7, z_peers, sum(n_group[k] for k in range(8)))
    arrive(d_copies)
    total[share_of(p), :] = sum(d_in[k].astype(f32) for k in range(4)).astype(bf)
    g_copies = [
        remote(total.at[share_of(p)], total.at[share_of(p)], g_send.at[k], g_recv.at[k], group[k])
        for k in range(7)
    ]
    along_y(0)
    arrive(n_copies)
    n_copies = spread(n_y, y, 10, y_peers, sum(n_z[k] for k in range(4)))
    along_y(1)
    scale = 1.0 / math.sqrt(2 * 64 * BLOCK)
    arrive(g_copies)
    arrive(n_copies)
    gain_total = sum(n_y[k] for k in range(4)) * scale
    for l in range(12):
        cut = slice(l * 128, l * 128 + 128)
        gk_ref[:, cut] = total[l * KER : l * KER + KER, :].astype(f32) * scale
        gg_ref[:, cut] = gain_total[l : l + 1, :]
    for i in range(2):
        arrive(y_copies[i])
        whole = sum(y_in[i, k].astype(f32) for k in range(4)) * scale
        gp_ref[:, i * 768 : i * 768 + 384] = whole[:24, :]
        gp_ref[:, i * 768 + 384 : i * 768 + 768] = whole[24:, :]
    gh_store.wait()
    out_store.wait()
    for to, sent in t_copies:

        @pl.when(z != to)
        def _():
            sent.wait_send()

    for copy in copies:
        copy.wait_send()


def finish_kernel(out, gh, gp, gk, gg, out_to, gh_to, gp_to, gk_to, gg_to, sem):
    pairs = ((out, out_to), (gh, gh_to), (gp, gp_to), (gk, gk_to))
    moves = [pltpu.make_async_copy(src, dst, sem.at[i]) for i, (src, dst) in enumerate(pairs)]
    for move in moves:
        move.start()
    gg_to[...] = gg[...].reshape(D)
    for move in moves:
        move.wait()


def layer(x, gain, w_key, w_value, w_query, w_out, gain_conv, taps, w_point, cot):
    bf, f32 = jnp.bfloat16, jnp.float32
    vmem = pl.BlockSpec(memory_space=pltpu.VMEM)
    hbm = pl.BlockSpec(memory_space=pl.ANY)
    dma = pltpu.SemaphoreType.DMA
    shapes = [((BLOCK, D), bf), ((BLOCK, D), bf), ((24, D), f32), ((KER, D), f32)]
    outs = [jax.ShapeDtypeStruct(*shape) for shape in shapes]
    scratch = [
        ((D, WIDE), bf), ((D, WIDE), bf), ((D, WIDE), bf), ((WIDE, D), bf), ((D, D), bf),
        ((BLOCK, D), bf),
        ((HEADS, 192, 128), bf), ((HEADS, 96, 128), bf),
        ((16, 208, HALF), bf), ((96, 1024), bf), ((112, 1024), f32), ((8, 1024), f32),
        ((96, 1024), bf), ((WIDE, 128), bf), ((8 * BLOCK, D), bf),
        ((BLOCK, D), bf), ((12, BLOCK, 128), f32), ((12, 160, 128), f32), ((12, BLOCK, 128), f32),
        ((12, 160, 128), f32), ((12, BLOCK, 128), f32), ((BLOCK, D), bf), ((D, BLOCK), f32),
        ((2, 8, 96, 128), bf), ((2, 96, 1024), bf), ((4, 16, D), bf), ((4, 16, D), bf),
        ((2, 4, 48, 768), bf), ((2, 4, 48, 768), bf), ((2, 2, 48, 384), bf), ((2, 4, 48, 384), bf),
        ((2, BLOCK, 128), f32), ((16, 128), f32), ((384, 128), bf), ((7, 48, 128), bf),
        ((4, 48, 128), bf), ((4, 48, 128), bf), ((384, 128), bf),
        ((8, 16, 128), f32), ((4, 16, 128), f32), ((4, 16, 128), f32),
        ((BLOCK, D), bf), ((BLOCK, D), bf),
    ]
    counts = [10, 8, 8, 8, 8, 8, 8, 14, 14, 8, 8, 4, 4, 14, 14, 7, 7, 3, 3, 3, 3, 7, 7, 8, 8, 6, 6]
    counts += [13, 13, 2]
    results = pl.pallas_call(
        layer_kernel,
        name="layer",
        out_shape=tuple(outs + [jax.ShapeDtypeStruct((1, D), f32)]),
        in_specs=[vmem, vmem, hbm, hbm, hbm, hbm, vmem, vmem, hbm, vmem],
        out_specs=(hbm, hbm, vmem, vmem, vmem),
        scratch_shapes=[pltpu.VMEM(*shape) for shape in scratch] + [dma((n,)) for n in counts],
        compiler_params=pltpu.CompilerParams(
            collective_id=0, has_side_effects=True, vmem_limit_bytes=60 << 20
        ),
        cost_estimate=pl.CostEstimate(
            flops=9 * 10**9, bytes_accessed=16 * 2**20, transcendentals=2**23
        ),
    )(x, gain, w_key, w_value, w_query, w_out, gain_conv, taps, w_point, cot)
    return pl.pallas_call(
        finish_kernel,
        name="finish",
        out_shape=tuple(outs + [jax.ShapeDtypeStruct((D,), f32)]),
        in_specs=[vmem] * 5,
        out_specs=(hbm,) * 4 + (vmem,),
        scratch_shapes=[dma((4,))],
    )(*results)


def on_device(
    inputs,
    attention_norm_gain,
    w_query,
    w_key,
    w_value,
    w_out,
    gain_conv,
    kernel,
    w_point,
    cotangent,
):
    layer_out, grad_hidden, grad_point, grad_kernel, grad_gain = layer(
        inputs[0], attention_norm_gain, w_key, w_value, w_query, w_out,
        gain_conv, kernel, w_point, cotangent[0],
    )
    return layer_out[None], grad_hidden[None], grad_point, grad_kernel, grad_gain


def solution(mesh):
    placed = (P("utt", "seq", None), P(), P(), P(), P(), P(), P(), P(), P(), P("utt", "seq", None))
    return jax.shard_map(
        on_device,
        mesh=mesh,
        in_specs=placed,
        out_specs=(P("utt", "seq", None), P("utt", "seq", None), P("seq", None), P(), P()),
        check_vma=False,
    )
```

```python
import math

import jax
import jax.numpy as jnp
from jax import lax
from jax.experimental import pallas as pl
from jax.experimental.pallas import tpu as pltpu
from jax.sharding import PartitionSpec as P

D = 1536
HEADS = 8
HEAD_DIM = 96
WIDE = HEADS * HEAD_DIM
KER = 32
BLOCK = 128
HALF = 512
LOG2E = 1.4426950408889634

OWN, SIB, ZM, ZP, Z2, SIB_ZM, SIB_ZP, SIB_Z2 = range(8)


def rows_norm(values):
    mean = jnp.mean(values, axis=-1, keepdims=True)
    centered = values - mean
    rstd = lax.rsqrt(jnp.mean(centered * centered, axis=-1, keepdims=True) + 1e-05)
    return centered * rstd, rstd


def matmul(a, b, da=1, db=0):
    return lax.dot_general(a, b, (((da,), (db,)), ((), ())), preferred_element_type=jnp.float32)


def layer_kernel(
    x_ref, gain_ref, wk_hbm, wv_hbm, wq_hbm, wo_hbm, gain_conv_ref, taps_hbm, wp_hbm, cot_hbm,
    out_ref, gh_ref, gp_ref, gk_ref, gg_ref,
    wk, wv, wq, wo, wp, normed, kv_out, q_out, kv, qt, acc, top, mix_out, mixt, cots,
    hidden, hhat, ci, back, dz, conv, act, act_t, act_out, act_in, edge, halo, tile_out, tile_in,
    y_out, y_in, part, gain_sum, b_out, b_in, c_in, d_in, total, n_group, n_z, n_y,
    gh_rows, out_rows, taps_ref,
    w_sem, kv_send, kv_recv, q_send, q_recv, m_send, m_recv, r_send, r_recv, s_send, s_recv,
    e_send, e_recv, a_send, a_recv, b_send, b_recv, c_send, c_recv, d_send, d_recv,
    g_send, g_recv, t_send, t_recv, y_send, y_recv, n_send, n_recv, o_sem,
):
    f32, bf = jnp.float32, jnp.bfloat16
    s = lax.axis_index("seq")
    u = lax.axis_index("utt")
    z, y_hi, x, c = s // 16, (s // 8) % 2, (s // 2) % 4, s % 2
    h, p, y = y_hi * 4 + x, s % 8, y_hi * 2 + u

    def dev(zz, hh, cc):
        return {"seq": zz * 16 + hh * 2 + cc}

    def plane(side, step, sign=1):
        return (y_hi + side) % 2 * 4 + (x + sign * step + 4) % 4

    near = [(0, 1), (0, 2), (0, 3)]
    away = [(1, 0), (1, 1), (1, 2), (1, 3)]
    up, down, sibling = dev((z + 1) % 4, h, c), dev((z + 3) % 4, h, c), dev(z, h, 1 - c)
    right, left = {"seq": (s + 1) % 64}, {"seq": (s + 63) % 64}
    group = [{"seq": s // 8 * 8 + (p + k) % 8} for k in range(1, 8)]
    z_peers = [dev((z + k) % 4, h, c) for k in range(1, 4)]
    y_peers = [
        {"seq": z * 16 + (y + k) % 4 // 2 * 8 + p, "utt": (y + k) % 4 % 2} for k in range(1, 4)
    ]
    copies = []

    def remote(src, dst, send, recv, to):
        copy = pltpu.make_async_remote_copy(
            src_ref=src, dst_ref=dst, send_sem=send, recv_sem=recv,
            device_id=to, device_id_type=pl.DeviceIdType.MESH,
        )
        copy.start()
        copies.append(copy)
        return copy

    def arrive(group_of_copies):
        for copy in group_of_copies:
            copy.wait_recv()

    loads = {}
    sem = 0
    for name, src, dst, cuts in (
        ("k", wk_hbm, wk, 2), ("v", wv_hbm, wv, 2), ("q", wq_hbm, wq, 2),
        ("p", wp_hbm, wp, 2), ("o", wo_hbm, wo, 2),
    ):
        rows = dst.shape[0] // cuts
        loads[name] = []
        for i in range(cuts):
            cut = pl.ds(i * rows, rows)
            loads[name].append(pltpu.make_async_copy(src.at[cut], dst.at[cut], w_sem.at[sem]))
            if name in "kvq":
                loads[name][-1].start()
            sem += 1

    own_rows = pl.ds(pl.multiple_of(p * BLOCK, BLOCK), BLOCK)
    late_loads = [
        pltpu.make_async_copy(cot_hbm, cots.at[own_rows], o_sem.at[2]),
        pltpu.make_async_copy(taps_hbm, taps_ref, o_sem.at[3]),
    ]

    def loaded(name):
        for load in loads[name]:
            load.wait()

    for slot in range(16):
        kv[slot, 192:208, :] = jnp.ones((16, HALF), bf)
    barrier = pltpu.get_barrier_semaphore()
    greeted = [dev(z, plane(a, b), c) for a, b in near + away] + group + z_peers + y_peers
    greeted += [right, left]
    for to in greeted:
        pl.semaphore_signal(barrier, inc=1, device_id=to, device_id_type=pl.DeviceIdType.MESH)

    xhat, unused_item = rows_norm(x_ref[...].astype(f32))
    normed[...] = (xhat * gain_ref[...].reshape(1, D)).astype(bf)
    loaded("k")
    rows = matmul(normed[...], wk[...]).T.astype(bf)
    for i in range(HEADS):
        kv_out[i, 0:96, :] = rows[i * 96 : i * 96 + 96, :]
    loaded("v")
    rows = matmul(normed[...], wv[...]).T.astype(bf)
    for i in range(HEADS):
        kv_out[i, 96:192, :] = rows[i * 96 : i * 96 + 96, :]
    pl.semaphore_wait(barrier, len(greeted))
    mine = pl.ds(pl.multiple_of(x * 128, 128), 128)
    lanes = pl.ds(pl.multiple_of(h * 128, 128), 128)

    def exchange(src, dst, send, recv, peers):
        made = []
        for a, b in peers:
            to = plane(a, b)
            made.append(remote(src(to), dst, send.at[4 * a + b], recv.at[4 * a + b], dev(z, to, c)))
        return made

    kv_near = exchange(lambda i: kv_out.at[i], kv.at[y_hi, 0:192, mine], kv_send, kv_recv, near)
    kv_away = exchange(lambda i: kv_out.at[i], kv.at[y_hi, 0:192, mine], kv_send, kv_recv, away)
    kv[y_hi, 0:192, mine] = kv_out[h]
    loaded("q")
    for load in late_loads + loads["p"] + loads["o"]:
        load.start()
    rows = (matmul(normed[...], wq[...]) * (LOG2E / math.sqrt(HEAD_DIM))).T.astype(bf)
    for i in range(HEADS):
        q_out[i] = rows[i * 96 : i * 96 + 96, :]
    q_near = exchange(lambda i: q_out.at[i], qt.at[:, lanes], q_send, q_recv, near)
    q_away = exchange(lambda i: q_out.at[i], qt.at[:, lanes], q_send, q_recv, away)
    qt[:, lanes] = q_out[h]
    acc[...] = jnp.zeros_like(acc)
    top[...] = jnp.full_like(top, -1e30)

    NEAR, AWAY = y_hi, 1 - y_hi
    hops = []

    def forward(slot, half, to, to_slot):
        i = len(hops)
        copy = remote(kv.at[2 * slot + half, 0:192], kv.at[2 * to_slot + half, 0:192],
                      r_send.at[i], r_recv.at[i], to)
        hops.append(copy)
        return copy

    def attend(side, *halves):
        span = pl.ds(pl.multiple_of(side * HALF, HALF), HALF)
        halves = [2 * slot + half for slot, half in halves]
        scores = [matmul(kv[i, 0:96, :], qt[:, span], 0, 0) for i in halves]
        before = top[0:1, span]
        newest = before
        for one in scores:
            newest = jnp.maximum(newest, jnp.max(one, axis=0, keepdims=True))
        result = acc[:, span] * jnp.exp2(before - newest)
        for i, one in zip(halves, scores):
            result += matmul(kv[i, 96:208, :], jnp.exp2(one - newest).astype(bf))
        acc[:, span] = result
        top[0:1, span] = newest

    def attend_both(*halves):
        def one_side(side, carry):
            attend(side, *halves)
            return carry

        lax.fori_loop(0, 2, one_side, 0)

    arrive(kv_near)
    zm_n = forward(OWN, NEAR, up, ZM)
    zp_n = forward(OWN, NEAR, down, ZP)
    sib_n = forward(OWN, NEAR, sibling, SIB)
    loaded("p")
    for load in late_loads:
        load.wait()
    grads = matmul(cots[own_rows, :], wp[...], 1, 1)
    for l in range(12):
        back[l] = grads[:, l * 128 : l * 128 + 128]
    arrive(kv_away)
    zp_a = forward(OWN, AWAY, down, ZP)
    zm_a = forward(OWN, AWAY, up, ZM)
    sib_a = forward(OWN, AWAY, sibling, SIB)
    arrive(q_near)
    sib_n.wait_recv()
    attend(NEAR, (OWN, NEAR), (SIB, NEAR))
    arrive(q_away)
    ahead, behind = dev(z, plane(0, 1), c), dev(z, plane(0, 3), c)

    def cot_rows(step, first=0, count=BLOCK):
        start = ((x + step) % 4 * 2 + c) * BLOCK + first
        return cots.at[pl.ds(pl.multiple_of(start, 64), count)]

    def cot_send(i, src, to):
        return remote(src, src, s_send.at[i], s_recv.at[i], to)

    cot_ahead = cot_send(0, cot_rows(0), ahead)
    cot_behind = cot_send(1, cot_rows(0), behind)
    cot_relays = [cot_send(2, cot_rows(0), sibling)]
    attend(AWAY, (OWN, NEAR), (SIB, NEAR))
    sib_a.wait_recv()
    attend_both((OWN, AWAY), (SIB, AWAY))
    zm_n.wait_recv()
    z2_n = forward(ZM, NEAR, up, Z2)
    szm_n = forward(ZM, NEAR, sibling, SIB_ZM)
    zp_n.wait_recv()
    szp_n = forward(ZP, NEAR, sibling, SIB_ZP)
    attend_both((ZM, NEAR), (ZP, NEAR))
    zp_a.wait_recv()
    z2_a = forward(ZP, AWAY, down, Z2)
    szp_a = forward(ZP, AWAY, sibling, SIB_ZP)
    zm_a.wait_recv()
    szm_a = forward(ZM, AWAY, sibling, SIB_ZM)
    arrive([szm_n, szp_n])
    attend_both((SIB_ZM, NEAR), (SIB_ZP, NEAR), (ZM, AWAY), (ZP, AWAY))
    z2_n.wait_recv()
    sz2_n = forward(Z2, NEAR, sibling, SIB_Z2)
    z2_a.wait_recv()
    sz2_a = forward(Z2, AWAY, sibling, SIB_Z2)
    arrive([szm_a, szp_a])
    cot_ahead.wait_recv()
    cot_first = cot_send(3, cot_rows(3, 0, 64), ahead)
    cot_behind.wait_recv()
    cot_second = cot_send(4, cot_rows(1, 64, 64), behind)
    cot_relays += [cot_send(5, cot_rows(3), sibling), cot_send(6, cot_rows(1), sibling)]
    attend_both((SIB_ZM, AWAY), (SIB_ZP, AWAY), (Z2, NEAR), (Z2, AWAY))
    arrive([sz2_n, sz2_a])
    band = pl.ds(pl.multiple_of(h * 96, 96), 96)

    def give_back(side, peers):
        span = pl.ds(pl.multiple_of(side * HALF, HALF), HALF)
        mix_out[:, span] = (acc[0:96, span] / acc[96:97, span]).astype(bf)
        return exchange(
            lambda i: mix_out.at[:, pl.ds(pl.multiple_of(i * 128, 128), 128)],
            mixt.at[band, :], m_send, m_recv, peers,
        )

    attend(AWAY, (SIB_Z2, NEAR), (SIB_Z2, AWAY))
    m_away = give_back(AWAY, away)
    attend(NEAR, (SIB_Z2, NEAR), (SIB_Z2, AWAY))
    m_near = give_back(NEAR, near)
    mixt[band, :] = mix_out[:, lanes]
    loaded("o")
    arrive(m_away + m_near)
    hidden[...] = (x_ref[...].astype(f32) + matmul(mixt[...], wo[...], 0, 0)).astype(bf)

    standard, rstd = rows_norm(hidden[...].astype(f32))
    conv_in = (standard * gain_conv_ref[...].reshape(1, D)).astype(bf)
    edge[0] = conv_in[BLOCK - 16 :, :]
    edge[1] = conv_in[:16, :]
    halos = [
        remote(edge.at[0], halo.at[0], e_send.at[0], e_recv.at[0], right),
        remote(edge.at[1], halo.at[1], e_send.at[1], e_recv.at[1], left),
    ]
    for l in range(12):
        hhat[l] = standard[:, l * 128 : l * 128 + 128]
        ci[l, 16:144, :] = conv_in[:, l * 128 : l * 128 + 128].astype(f32)

    def place_halo(ref, slot):
        low = jnp.where(s > 0, halo[slot].astype(f32), 0.0)
        high = jnp.where(s < 63, halo[slot + 1].astype(f32), 0.0)
        for l in range(12):
            ref[l, 0:16, :] = low[:, l * 128 : l * 128 + 128]
            ref[l, 144:160, :] = high[:, l * 128 : l * 128 + 128]

    def span_of(l):
        return pl.ds(pl.multiple_of(l * 128, 128), 128)

    def conv_rows(l, first, count):
        result = jnp.zeros((count, 128), f32)
        for j in range(KER):
            result += taps_ref[j : j + 1, span_of(l)] * ci[l, first + j : first + j + count, :]
        conv[l, first : first + count, :] = result

    def grad_rows(l, first, count):
        result = jnp.zeros((count, 128), f32)
        for j in range(KER):
            start = first + 32 - j
            result += taps_ref[j : j + 1, span_of(l)] * dz[l, start : start + count, :]
        return result

    def middle(l, carry):
        conv_rows(l, 16, 96)
        return carry

    lax.fori_loop(0, 12, middle, 0)
    arrive([cot_first, cot_second])
    cot_relays.append(cot_send(7, cot_rows(2), sibling))
    arrive(halos)
    place_halo(ci, 0)

    def activate(l, carry):
        conv_rows(l, 0, 16)
        conv_rows(l, 112, 16)
        value = conv[l]
        sig = 1.0 / (1.0 + jnp.exp(-value))
        rounded = (value * sig).astype(bf)
        act[:, span_of(l)] = rounded
        act_t[span_of(l), :] = rounded.astype(f32).T
        dz[l, 16:144, :] = back[l] * (sig * (1.0 + value * (1.0 - sig)))
        return carry

    own_lanes = pl.ds(pl.multiple_of(p * 128, 128), 128)
    act_copies = []

    def send_act(i):
        for to in range(8):
            starts = [24 * (8 * b + to) for b in range(4 * i, 4 * i + 4)]
            pieces = [act_t[start : start + 24, :] for start in starts]
            act_out[i, to] = jnp.concatenate(pieces, axis=0).astype(bf)
        act_copies.append([
            remote(act_out.at[i, (p + k) % 8], act_in.at[i, :, own_lanes],
                   a_send.at[7 * i + k - 1], a_recv.at[7 * i + k - 1], group[k - 1])
            for k in range(1, 8)
        ])
        act_in[i, :, own_lanes] = act_out[i, p]

    lax.fori_loop(0, 6, activate, 0)
    send_act(0)
    lax.fori_loop(6, 12, activate, 0)
    for l in range(12):
        edge[2, :, l * 128 : l * 128 + 128] = dz[l, 128:144, :].astype(bf)
        edge[3, :, l * 128 : l * 128 + 128] = dz[l, 16:32, :].astype(bf)
    halos = [
        remote(edge.at[2], halo.at[2], e_send.at[2], e_recv.at[2], right),
        remote(edge.at[3], halo.at[3], e_send.at[3], e_recv.at[3], left),
    ]
    send_act(1)

    def taps_grad(l, carry):
        grad = dz[l, 16:144, :]
        for j0 in range(0, KER, 16):
            rows = [
                jnp.sum(grad * ci[l, j : j + BLOCK, :], axis=0, keepdims=True)
                for j in range(j0, j0 + 16)
            ]
            at = pl.ds(pl.multiple_of(l * KER + j0, 16), 16)
            b_out[at, :] = jnp.concatenate(rows, axis=0).astype(bf)
        return carry

    lax.fori_loop(0, 12, taps_grad, 0)
    share = 12 * KER // 8

    def share_of(i):
        return pl.ds(pl.multiple_of(i * share, share), share)

    b_copies = [
        remote(b_out.at[share_of((p + k) % 8)], b_in.at[k - 1],
               b_send.at[k - 1], b_recv.at[k - 1], group[k - 1])
        for k in range(1, 8)
    ]

    def spread(ref, at, base, peers, value):
        ref[at] = value
        return [
            remote(ref.at[at], ref.at[at], n_send.at[base + k], n_recv.at[base + k], to)
            for k, to in enumerate(peers)
        ]

    t_copies = []

    def tile_rows(i):
        arrive(act_copies[i])
        for j in range(2):
            tile = matmul(act_in[i], cots[:, j * 768 : j * 768 + 768])
            for b in range(2):
                tile_out[j, 2 * i + b] = tile[48 * b : 48 * b + 48, :].astype(bf)
            for b in range(2):
                to = 2 * i + b
                sent = pltpu.make_async_remote_copy(
                    src_ref=tile_out.at[j, to], dst_ref=tile_in.at[j, z],
                    send_sem=t_send.at[4 * j + to], recv_sem=t_recv.at[4 * j + z],
                    device_id=dev(to, h, c), device_id_type=pl.DeviceIdType.MESH,
                )
                t_copies.append((to, sent))

                @pl.when(z != to)
                def _():
                    sent.start()

    y_copies = []

    def along_y(i):
        for k in range(4):
            got = pltpu.make_async_remote_copy(
                src_ref=tile_out.at[i, k], dst_ref=tile_in.at[i, k],
                send_sem=t_send.at[4 * i + k], recv_sem=t_recv.at[4 * i + k],
                device_id=dev(k, h, c), device_id_type=pl.DeviceIdType.MESH,
            )

            @pl.when(z != k)
            def _():
                got.wait_recv()

        tile_in[i, z] = tile_out[i, z]
        mixed = sum(tile_in[i, k].astype(f32) for k in range(4))
        for b in range(2):
            rows = mixed[24 * b : 24 * b + 24, :]
            y_out[i, b] = jnp.concatenate([rows[:, :384], rows[:, 384:]], axis=0).astype(bf)
        y_copies.append([
            remote(y_out.at[i, (y + k) % 4 // 2], y_in.at[i, y],
                   y_send.at[3 * i + k - 1], y_recv.at[3 * i + k - 1], y_peers[k - 1])
            for k in range(1, 4)
        ])
        y_in[i, y] = y_out[i, y_hi]

    out_rows[...] = (hidden[...].astype(f32) + matmul(act[...], wp[...])).astype(bf)
    out_store = pltpu.make_async_copy(out_rows, out_ref, o_sem.at[1])
    out_store.start()
    arrive(cot_relays)
    tile_rows(0)
    arrive(b_copies)
    c_in[z] = sum([b_out[share_of(p), :].astype(f32)] + [b_in[k].astype(f32) for k in range(7)]).astype(bf)
    c_copies = [
        remote(c_in.at[z], c_in.at[z], c_send.at[k], c_recv.at[k], z_peers[k]) for k in range(3)
    ]
    tile_rows(1)
    arrive(halos)
    place_halo(dz, 2)
    part[...] = jnp.zeros_like(part)
    gain_sum[...] = jnp.zeros_like(gain_sum)

    def backward(l, carry):
        grad = grad_rows(l, 0, BLOCK)
        gain_sum[pl.ds(l, 1), :] = jnp.sum(grad * hhat[l], axis=0, keepdims=True)
        g = grad * gain_conv_ref[span_of(l)].reshape(1, 128)
        back[l] = g
        part[0] += g
        part[1] += g * hhat[l]
        return carry

    lax.fori_loop(0, 12, backward, 0)

    n_copies = spread(n_group, p, 0, group, gain_sum[...])
    arrive(c_copies)
    d_in[y] = sum(c_in[k].astype(f32) for k in range(4)).astype(bf)
    d_copies = [
        remote(d_in.at[y], d_in.at[y], d_send.at[k], d_recv.at[k], y_peers[k]) for k in range(3)
    ]
    mean_g = jnp.sum(part[0], axis=-1, keepdims=True) * (1.0 / D)
    mean_gh = jnp.sum(part[1], axis=-1, keepdims=True) * (1.0 / D)
    for l in range(12):
        cut = slice(l * 128, l * 128 + 128)
        inner = back[l] - mean_g - hhat[l] * mean_gh
        gh_rows[:, cut] = (cots[own_rows, cut].astype(f32) + rstd * inner).astype(bf)
    gh_store = pltpu.make_async_copy(gh_rows, gh_ref, o_sem.at[0])
    gh_store.start()
    arrive(n_copies)
    n_copies = spread(n_z, z, 7, z_peers, sum(n_group[k] for k in range(8)))
    arrive(d_copies)
    total[share_of(p), :] = sum(d_in[k].astype(f32) for k in range(4)).astype(bf)
    g_copies = [
        remote(total.at[share_of(p)], total.at[share_of(p)], g_send.at[k], g_recv.at[k], group[k])
        for k in range(7)
    ]
    along_y(0)
    arrive(n_copies)
    n_copies = spread(n_y, y, 10, y_peers, sum(n_z[k] for k in range(4)))
    along_y(1)
    scale = 1.0 / math.sqrt(2 * 64 * BLOCK)
    arrive(g_copies)
    arrive(n_copies)
    gain_total = sum(n_y[k] for k in range(4)) * scale
    for l in range(12):
        cut = slice(l * 128, l * 128 + 128)
        gk_ref[:, cut] = total[l * KER : l * KER + KER, :].astype(f32) * scale
        gg_ref[:, cut] = gain_total[l : l + 1, :]
    for i in range(2):
        arrive(y_copies[i])
        whole = sum(y_in[i, k].astype(f32) for k in range(4)) * scale
        gp_ref[:, i * 768 : i * 768 + 384] = whole[:24, :]
        gp_ref[:, i * 768 + 384 : i * 768 + 768] = whole[24:, :]
    gh_store.wait()
    out_store.wait()
    for to, sent in t_copies:

        @pl.when(z != to)
        def _():
            sent.wait_send()

    for copy in copies:
        copy.wait_send()


def finish_kernel(out, gh, gp, gk, gg, out_to, gh_to, gp_to, gk_to, gg_to, sem):
    pairs = ((out, out_to), (gh, gh_to), (gp, gp_to), (gk, gk_to))
    moves = [pltpu.make_async_copy(src, dst, sem.at[i]) for i, (src, dst) in enumerate(pairs)]
    for move in moves:
        move.start()
    gg_to[...] = gg[...].reshape(D)
    for move in moves:
        move.wait()


def layer(x, gain, w_key, w_value, w_query, w_out, gain_conv, taps, w_point, cot):
    bf, f32 = jnp.bfloat16, jnp.float32
    vmem = pl.BlockSpec(memory_space=pltpu.VMEM)
    hbm = pl.BlockSpec(memory_space=pl.ANY)
    dma = pltpu.SemaphoreType.DMA
    shapes = [((BLOCK, D), bf), ((BLOCK, D), bf), ((24, D), f32), ((KER, D), f32)]
    outs = [jax.ShapeDtypeStruct(*shape) for shape in shapes]
    scratch = [
        ((D, WIDE), bf), ((D, WIDE), bf), ((D, WIDE), bf), ((WIDE, D), bf), ((D, D), bf),
        ((BLOCK, D), bf),
        ((HEADS, 192, 128), bf), ((HEADS, 96, 128), bf),
        ((16, 208, HALF), bf), ((96, 1024), bf), ((112, 1024), f32), ((8, 1024), f32),
        ((96, 1024), bf), ((WIDE, 128), bf), ((8 * BLOCK, D), bf),
        ((BLOCK, D), bf), ((12, BLOCK, 128), f32), ((12, 160, 128), f32), ((12, BLOCK, 128), f32),
        ((12, 160, 128), f32), ((12, BLOCK, 128), f32), ((BLOCK, D), bf), ((D, BLOCK), f32),
        ((2, 8, 96, 128), bf), ((2, 96, 1024), bf), ((4, 16, D), bf), ((4, 16, D), bf),
        ((2, 4, 48, 768), bf), ((2, 4, 48, 768), bf), ((2, 2, 48, 384), bf), ((2, 4, 48, 384), bf),
        ((2, BLOCK, 128), f32), ((16, 128), f32), ((384, 128), bf), ((7, 48, 128), bf),
        ((4, 48, 128), bf), ((4, 48, 128), bf), ((384, 128), bf),
        ((8, 16, 128), f32), ((4, 16, 128), f32), ((4, 16, 128), f32),
        ((BLOCK, D), bf), ((BLOCK, D), bf), ((KER, D), f32),
    ]
    counts = [10, 8, 8, 8, 8, 8, 8, 14, 14, 8, 8, 4, 4, 14, 14, 7, 7, 3, 3, 3, 3, 7, 7, 8, 8, 6, 6]
    counts += [13, 13, 4]
    results = pl.pallas_call(
        layer_kernel,
        name="layer",
        out_shape=tuple(outs + [jax.ShapeDtypeStruct((1, D), f32)]),
        in_specs=[vmem, vmem, hbm, hbm, hbm, hbm, vmem, hbm, hbm, hbm],
        out_specs=(hbm, hbm, vmem, vmem, vmem),
        scratch_shapes=[pltpu.VMEM(*shape) for shape in scratch] + [dma((n,)) for n in counts],
        compiler_params=pltpu.CompilerParams(
            collective_id=0, has_side_effects=True, vmem_limit_bytes=60 << 20
        ),
        cost_estimate=pl.CostEstimate(
            flops=9 * 10**9, bytes_accessed=16 * 2**20, transcendentals=2**23
        ),
    )(x, gain, w_key, w_value, w_query, w_out, gain_conv, taps, w_point, cot)
    return pl.pallas_call(
        finish_kernel,
        name="finish",
        out_shape=tuple(outs + [jax.ShapeDtypeStruct((D,), f32)]),
        in_specs=[vmem] * 5,
        out_specs=(hbm,) * 4 + (vmem,),
        scratch_shapes=[dma((4,))],
    )(*results)


def on_device(
    inputs,
    attention_norm_gain,
    w_query,
    w_key,
    w_value,
    w_out,
    gain_conv,
    kernel,
    w_point,
    cotangent,
):
    layer_out, grad_hidden, grad_point, grad_kernel, grad_gain = layer(
        inputs[0], attention_norm_gain, w_key, w_value, w_query, w_out,
        gain_conv, kernel, w_point, cotangent[0],
    )
    return layer_out[None], grad_hidden[None], grad_point, grad_kernel, grad_gain


def solution(mesh):
    placed = (P("utt", "seq", None), P(), P(), P(), P(), P(), P(), P(), P(), P("utt", "seq", None))
    return jax.shard_map(
        on_device,
        mesh=mesh,
        in_specs=placed,
        out_specs=(P("utt", "seq", None), P("utt", "seq", None), P("seq", None), P(), P()),
        check_vma=False,
    )
```
